128 devices in a mesh: group: 4 (over x), blk: 32 (over z, y, core).
Axes of the slice: x: 4, y: 4, z: 4, core: 2. Of those that a mesh axis runs over, the one named last changes fastest.
Arguments:
- embeddings: bfloat16 [32768, 1024], P(('group', 'blk'))
- cluster: int32 [32768], P(('group', 'blk')), may hold values from 0 to 7, as said below
- row_index: int32 [32768], P(('group', 'blk')), may hold values from 0 to 32767, each once
Outputs:
- nearest: float32 [32768], P(('group', 'blk'))
The draws below stay inside these ranges and needn't reach their ends.
Inputs may be any that keep to these rules, and one draw needn't show every extreme that they name: `cluster`: cluster c belongs to owner group c // 2. The rows of one device hold at most 128 rows of one owner group; in every device's rows exactly one owner group has 128 rows, the same group for all devices with the same blk index.
All inputs are finite; a program needn't handle non-finite values.
Results may differ from the reference program's by a relative error of at most 0.00046.
Values may be sent and summed in bfloat16 or wider, within the bound.
No kernel may reach another device: no remote copies, remote signals or barrier semaphores. Data moves between devices by JAX's collectives and lax.ppermute only.
A program may use at most 64 MiB of HBM per device.

```python
import jax
import jax.numpy as jnp
from jax import lax

E = 1024
ROW_DEV = 256
CL_GROUP = 2
OWNERS = 4
CYCLE = 32
CAP = 128
ROWS = 32768
GBOUND = 16384


def cluster_draw(base_key):
    folded = jax.random.fold_in(base_key, 11)
    key_hot, key_score, key_shuffle, key_local = jax.random.split(folded, 4)
    block_total = ROWS // ROW_DEV
    slot_total = OWNERS * CAP
    hot_groups = jax.random.randint(key_hot, (CYCLE,), 0, OWNERS)
    block_hot = hot_groups[jnp.arange(block_total, dtype=jnp.int32) % CYCLE]
    slot_group = jnp.arange(slot_total, dtype=jnp.int32) // CAP
    scores = jax.random.randint(key_score, (block_total, slot_total), 0, 65536) * slot_total
    scores = scores + jnp.arange(slot_total, dtype=jnp.int32)[None, :]
    scores = scores + jnp.where(slot_group[None, :] == block_hot[:, None], 1 << 28, 0)
    chosen = lax.top_k(scores, ROW_DEV)[1]
    groups = chosen // CAP
    shuffle_keys = jax.random.split(key_shuffle, block_total)
    groups = jax.vmap(jax.random.permutation)(shuffle_keys, groups)
    local_keys = jax.random.split(key_local, 3)
    first = jax.random.randint(local_keys[0], (block_total, ROW_DEV), 0, CL_GROUP)
    second = jax.random.randint(local_keys[1], (block_total, ROW_DEV), 0, CL_GROUP)
    third = jax.random.randint(local_keys[2], (block_total, ROW_DEV), 0, CL_GROUP)
    local_ids = jnp.minimum(jnp.minimum(first, second), third)
    return (groups * CL_GROUP + local_ids).reshape(ROWS).astype(jnp.int32)


def draw_cluster(key, part):
    return cluster_draw(key)


def draw_embeddings(key, part):
    clusters = cluster_draw(key)
    folded = jax.random.fold_in(key, 5)
    keys = jax.random.split(folded, 6)
    sub_pick = jax.random.randint(keys[0], (ROWS,), 0, 4)
    centre_weight = jax.random.uniform(keys[1], (ROWS, 1), minval=0.0, maxval=1.2)
    sub_weight = jax.random.uniform(keys[5], (ROWS, 1), minval=0.3, maxval=2.0)
    centres = jax.vmap(lambda cluster_id: jax.random.normal(jax.random.fold_in(keys[2], cluster_id), (E,)))(clusters)
    subs = jax.vmap(lambda sub_id: jax.random.normal(jax.random.fold_in(keys[3], sub_id), (E,)))(clusters * 4 + sub_pick)
    noise = jax.random.normal(keys[4], (ROWS, E))
    mixed = centre_weight * centres + sub_weight * subs + noise
    return mixed.astype(jnp.float32).astype(jnp.bfloat16)


def setup_inputs(seed: int = 0) -> dict:
    key_of = jax.random.split(jax.random.key(seed), 4)
    return {
        "embeddings": draw_embeddings(jax.random.fold_in(key_of[3], 71), 0),
        "cluster": draw_cluster(jax.random.fold_in(key_of[3], 71), 0),
        "row_index": jax.random.permutation(key_of[2], ROWS).astype(jnp.int32),
    }


EPSILON = 1e-06

def unit_rows(embeddings):
    widened = embeddings.astype(jnp.float32)
    scale_inv = lax.rsqrt(lax.optimization_barrier(jnp.sum(widened * widened, axis=1, keepdims=True)) + EPSILON)
    return (widened * scale_inv).astype(jnp.bfloat16)

def reference(embeddings, cluster, row_index):
    normed = unit_rows(embeddings)
    sort_keys = cluster * ROWS + row_index
    permuted = jnp.argsort(sort_keys).astype(jnp.int32)
    sorted_unit = normed[permuted].astype(jnp.float32)
    sorted_cluster = cluster[permuted]
    sorted_index = row_index[permuted]
    padded_unit = jnp.concatenate([jnp.zeros((GBOUND, E), jnp.float32), sorted_unit], axis=0)
    padded_cluster = jnp.concatenate([jnp.full((GBOUND,), -2, jnp.int32), sorted_cluster])
    padded_index = jnp.concatenate([jnp.zeros((GBOUND,), jnp.int32), sorted_index])
    block_rows = 512

    def block_best(block_number):
        start = (block_number * block_rows).astype(jnp.int32)
        left_unit = lax.dynamic_slice_in_dim(sorted_unit, start, block_rows, 0)
        left_cluster = lax.dynamic_slice_in_dim(sorted_cluster, start, block_rows, 0)
        left_index = lax.dynamic_slice_in_dim(sorted_index, start, block_rows, 0)
        window_unit = lax.dynamic_slice_in_dim(padded_unit, start, GBOUND + block_rows, 0)
        window_cluster = lax.dynamic_slice_in_dim(padded_cluster, start, GBOUND + block_rows, 0)
        window_index = lax.dynamic_slice_in_dim(padded_index, start, GBOUND + block_rows, 0)
        scores = jnp.dot(left_unit, window_unit.T, precision=lax.Precision.HIGHEST, preferred_element_type=jnp.float32)
        allowed = (left_cluster[:, None] == window_cluster[None, :]) & (window_index[None, :] < left_index[:, None])
        return lax.optimization_barrier(jnp.max(jnp.where(allowed, scores, jnp.float32(-1.0)), axis=1))
    results = lax.map(block_best, jnp.arange(ROWS // block_rows, dtype=jnp.int32))
    flat_best = results.reshape(ROWS)
    return jnp.zeros((ROWS,), jnp.float32).at[permuted].set(flat_best)
```

```python
import functools

import jax
import jax.numpy as jnp
from jax import lax
from jax.experimental import pallas as pl
from jax.experimental.pallas import tpu as pltpu
from jax.sharding import Mesh, PartitionSpec as P

CL_GROUP = 2
EPSILON = 1e-06
ROWS = 256
WIDTH = 1024
PAD = 16
SIZES = (4, 4, 4, 2)
AXES = ("x", "z", "y", "c")


def flat(x, z, y, c):
    return ((x % 4 * 4 + z % 4) * 4 + y % 4) * 2 + c


def fetch(unit, x=0, y=0, z=0, core=0):
    route = []
    for i in range(4):
        for j in range(4):
            for k in range(4):
                for c in range(2):
                    route.append((flat(i + x, j + z, k + y, c ^ core), flat(i, j, k, c)))
    return lax.ppermute(unit, AXES, route)


def give(values, x=0, y=0, z=0):
    return fetch(values, -x, -y, -z)


def pack_kernel(emb_ref, cluster_ref, index_ref, unit_ref):
    widened = emb_ref[...].astype(jnp.float32)
    scale = lax.rsqrt(jnp.sum(widened * widened, axis=1, keepdims=True) + EPSILON)
    unit_ref[0:ROWS, :] = (widened * scale).astype(jnp.bfloat16)
    cluster = cluster_ref[...]
    index = index_ref[...]
    high = lax.shift_right_logical(index, 8)
    low = index - high * 256
    ids = jnp.concatenate([low, high, cluster, jnp.zeros_like(low)], axis=1).astype(jnp.float32)
    ids = jnp.concatenate([ids, jnp.zeros((PAD - 1, WIDTH), jnp.float32)], axis=0)
    unit_ref[ROWS : ROWS + PAD, :] = ids.astype(jnp.bfloat16)


def pack(embeddings, cluster, row_index):
    return pl.pallas_call(
        pack_kernel,
        out_shape=jax.ShapeDtypeStruct((ROWS + PAD, WIDTH), jnp.bfloat16),
        in_specs=[pl.BlockSpec(memory_space=pltpu.VMEM)] * 3,
        out_specs=pl.BlockSpec(memory_space=pltpu.VMEM),
        cost_estimate=pl.CostEstimate(flops=4 * ROWS * WIDTH, bytes_accessed=4 * ROWS * WIDTH, transcendentals=ROWS),
    )(embeddings, cluster.reshape(1, ROWS), row_index.reshape(1, ROWS))


def ids_of(unit_ref):
    ids = unit_ref[ROWS : ROWS + PAD, :].astype(jnp.float32)[0:1, :]
    order = ids[:, 256:512] * 256.0 + ids[:, 0:256]
    return ids[:, 512:768], order


def compare_kernel(n_left, modes, n_prior, *refs):
    left = refs[:n_left]
    right = refs[n_left : n_left + len(modes)]
    prior = refs[n_left + len(modes) : n_left + len(modes) + n_prior]
    rest = refs[n_left + len(modes) + n_prior :]
    any_rows = any(m in ("both", "rows") for m in modes)
    row_out = rest[0] if any_rows else None
    col_outs = rest[1 if any_rows else 0 : (1 if any_rows else 0) + sum(m != "rows" for m in modes)]
    row_acc = rest[-1]
    low = jnp.float32(-1.0)
    keys = []
    for u in range(n_left):
        cluster, order = ids_of(left[u])
        turned = jnp.concatenate([cluster, order, jnp.zeros((6, ROWS), jnp.float32)], axis=0).T
        keys.append((turned[:, 0:1], turned[:, 1:2]))
    done_rows = [False] * n_left
    col = 0
    for r, mode in enumerate(modes):
        right_cluster, right_order = ids_of(right[r])
        col_best = None
        for u in range(n_left):
            scores = lax.dot_general(
                left[u][0:ROWS, :], right[r][0:ROWS, :], (((1,), (1,)), ((), ())), preferred_element_type=jnp.float32
            )
            left_cluster, left_order = keys[u]
            same = left_cluster == right_cluster
            scores = jnp.where(same, scores, low)
            if mode in ("both", "rows"):
                earlier = right_order < left_order
                part = jnp.where(earlier, scores, low)
                part = jnp.maximum(part[:, 0:128], part[:, 128:256])
                row_acc[u] = jnp.maximum(row_acc[u], part) if done_rows[u] else part
                done_rows[u] = True
            if mode in ("both", "cols"):
                later = left_order < right_order
                part = jnp.where(later, scores, low)
                part = jnp.max(part.reshape(ROWS // 8, 8, ROWS), axis=0)
                col_best = part if col_best is None else jnp.maximum(col_best, part)
        if mode in ("both", "cols"):
            col_outs[col][...] = jnp.max(col_best, axis=0, keepdims=True)
            col += 1
    if any_rows:
        for u in range(n_left):
            best = jnp.max(row_acc[u].T, axis=0, keepdims=True)
            if n_prior:
                best = jnp.maximum(best, prior[0][u : u + 1, :])
            row_out[u : u + 1, :] = best


def compare(left, right, modes, prior=None):
    n_left = len(left)
    outs = []
    if any(m in ("both", "rows") for m in modes):
        outs.append(jax.ShapeDtypeStruct((n_left, ROWS), jnp.float32))
    outs += [jax.ShapeDtypeStruct((1, ROWS), jnp.float32) for m in modes if m != "rows"]
    args = list(left) + list(right) + ([prior] if prior is not None else [])
    return pl.pallas_call(
        functools.partial(compare_kernel, n_left, tuple(modes), int(prior is not None)),
        out_shape=outs,
        in_specs=[pl.BlockSpec(memory_space=pltpu.VMEM)] * len(args),
        out_specs=[pl.BlockSpec(memory_space=pltpu.VMEM)] * len(outs),
        scratch_shapes=[pltpu.VMEM((n_left, ROWS, 128), jnp.float32)],
        compiler_params=pltpu.CompilerParams(vmem_limit_bytes=24 * 1024 * 1024),
        cost_estimate=pl.CostEstimate(
            flops=2 * n_left * len(modes) * ROWS * ROWS * WIDTH, bytes_accessed=2 * ROWS * WIDTH * len(args), transcendentals=0
        ),
    )(*args)


def on_device(embeddings, cluster, row_index):
    own = pack(embeddings, cluster, row_index)
    line = [own, fetch(own, x=1), fetch(own, x=2), fetch(own, x=-1)]
    p10 = fetch(own, y=1)
    p01 = fetch(own, z=1)
    pmm = fetch(own, y=-1, z=-1)
    pm1 = fetch(p01, y=-1)
    pm2 = fetch(pmm, z=-1)
    p21 = fetch(p10, y=1, z=1)
    p20 = fetch(p10, y=1)
    p02 = fetch(p01, z=1)
    p22 = fetch(pm2, y=-1)
    twin = [fetch(u, core=1) for u in line]
    left = line + twin
    rows1, own_best, c10, c01, cmm = compare(left, [own, p10, p01, pmm], ["cols", "both", "both", "both"])
    rows2, cm1, cm2, c21 = compare(left, [pm1, pm2, p21], ["both"] * 3, rows1)
    c20, c02, c22 = compare(left, [p20, p02, p22], ["cols"] * 3)
    got = [
        own_best,
        give(c10, y=1),
        give(c01, z=1),
        give(cmm, y=-1, z=-1),
        give(cm1, y=-1, z=1),
        give(cm2, y=-1, z=2),
        give(c21, y=2, z=1),
        give(c20, y=2),
        give(c02, z=2),
        give(c22, y=2, z=2),
    ]
    merged = jnp.maximum(rows2[0:4], fetch(rows2[4:8], core=1))
    got += [merged[0:1], give(merged[1:2], x=1), give(merged[2:3], x=2), give(merged[3:4], x=-1)]
    return functools.reduce(jnp.maximum, got).reshape(ROWS)


def solution(mesh):
    fine = Mesh(mesh.devices.reshape(SIZES), AXES)
    return jax.shard_map(
        on_device,
        mesh=fine,
        in_specs=(P(AXES, None), P(AXES), P(AXES)),
        out_specs=P(AXES),
        check_vma=False,
    )
```

```python
import functools

import jax
import jax.numpy as jnp
from jax import lax
from jax.experimental import pallas as pl
from jax.experimental.pallas import tpu as pltpu
from jax.sharding import Mesh, PartitionSpec as P

CL_GROUP = 2
EPSILON = 1e-06
ROWS = 256
WIDTH = 1024
PAD = 16
SIZES = (4, 4, 4, 2)
AXES = ("x", "z", "y", "c")


def flat(x, z, y, c):
    return ((x % 4 * 4 + z % 4) * 4 + y % 4) * 2 + c


def fetch(unit, x=0, y=0, z=0, core=0):
    route = []
    for i in range(4):
        for j in range(4):
            for k in range(4):
                for c in range(2):
                    route.append((flat(i + x, j + z, k + y, c ^ core), flat(i, j, k, c)))
    return lax.ppermute(unit, AXES, route)


def give(values, x=0, y=0, z=0):
    return fetch(values, -x, -y, -z)


def pack_kernel(emb_ref, cluster_ref, index_ref, unit_ref):
    widened = emb_ref[...].astype(jnp.float32)
    scale = lax.rsqrt(jnp.sum(widened * widened, axis=1, keepdims=True) + EPSILON)
    unit_ref[0:ROWS, :] = (widened * scale).astype(jnp.bfloat16)
    cluster = cluster_ref[...]
    index = index_ref[...]
    high = lax.shift_right_logical(index, 8)
    low = index - high * 256
    ids = jnp.concatenate([low, high, cluster, jnp.zeros_like(low)], axis=1).astype(jnp.float32)
    ids = jnp.concatenate([ids, jnp.zeros((PAD - 1, WIDTH), jnp.float32)], axis=0)
    unit_ref[ROWS : ROWS + PAD, :] = ids.astype(jnp.bfloat16)


def pack(embeddings, cluster, row_index):
    return pl.pallas_call(
        pack_kernel,
        out_shape=jax.ShapeDtypeStruct((ROWS + PAD, WIDTH), jnp.bfloat16),
        in_specs=[pl.BlockSpec(memory_space=pltpu.VMEM)] * 3,
        out_specs=pl.BlockSpec(memory_space=pltpu.VMEM),
        cost_estimate=pl.CostEstimate(flops=4 * ROWS * WIDTH, bytes_accessed=4 * ROWS * WIDTH, transcendentals=ROWS),
    )(embeddings, cluster.reshape(1, ROWS), row_index.reshape(1, ROWS))


def ids_of(unit_ref):
    ids = unit_ref[ROWS : ROWS + PAD, :].astype(jnp.float32)[0:1, :]
    order = ids[:, 256:512] * 256.0 + ids[:, 0:256]
    return ids[:, 512:768], order


def compare_kernel(left_slots, right_slots, tiles, n_left, n_right, has_rows, has_cols, *refs):
    left = refs[:n_left]
    right = refs[n_left : n_left + n_right]
    rest = list(refs[n_left + n_right :])
    row_prior = [rest.pop(0) if h else None for h in has_rows]
    col_prior = [rest.pop(0) if h else None for h in has_cols]
    row_outs = [rest.pop(0) if s else None for s in left_slots]
    col_outs = [rest.pop(0) if s else None for s in right_slots]
    row_acc = rest.pop(0)
    low = jnp.float32(-1.0)
    keys = []
    for u in range(n_left):
        cluster, order = ids_of(left[u])
        turned = jnp.concatenate([cluster, order, jnp.zeros((6, ROWS), jnp.float32)], axis=0).T
        keys.append((turned[:, 0:1], turned[:, 1:2]))
    seen = [False] * n_left
    for r in range(n_right):
        right_cluster, right_order = ids_of(right[r])
        col_best = None
        for u, v, rows, cols in tiles:
            if v != r:
                continue
            scores = lax.dot_general(
                left[u][0:ROWS, :], right[r][0:ROWS, :], (((1,), (1,)), ((), ())), preferred_element_type=jnp.float32
            )
            left_cluster, left_order = keys[u]
            scores = jnp.where(left_cluster == right_cluster, scores, low)
            if rows:
                part = jnp.where(right_order < left_order, scores, low)
                part = jnp.maximum(part[:, 0:128], part[:, 128:256])
                row_acc[u] = jnp.maximum(row_acc[u], part) if seen[u] else part
                seen[u] = True
            if cols:
                part = jnp.where(left_order < right_order, scores, low)
                part = jnp.max(part.reshape(ROWS // 8, 8, ROWS), axis=0)
                col_best = part if col_best is None else jnp.maximum(col_best, part)
        if right_slots[r]:
            best = jnp.max(col_best, axis=0, keepdims=True)
            col_outs[r][...] = jnp.maximum(best, col_prior[r][...]) if has_cols[r] else best
    for u in range(n_left):
        if left_slots[u]:
            best = jnp.max(row_acc[u].T, axis=0, keepdims=True)
            row_outs[u][...] = jnp.maximum(best, row_prior[u][...]) if has_rows[u] else best


def compare(left, right, pairs, rows=None, cols=None):
    rows, cols = rows or {}, cols or {}
    left_names, right_names = list(left), list(right)
    tiles = [(left_names.index(a), right_names.index(b), m != "cols", m != "rows") for a, b, m in pairs]
    left_slots = [any(t[0] == i and t[2] for t in tiles) for i in range(len(left))]
    right_slots = [any(t[1] == i and t[3] for t in tiles) for i in range(len(right))]
    has_rows = [n in rows and s for n, s in zip(left_names, left_slots)]
    has_cols = [n in cols and s for n, s in zip(right_names, right_slots)]
    args = [*left.values(), *right.values()]
    args += [rows[n] for n, h in zip(left_names, has_rows) if h]
    args += [cols[n] for n, h in zip(right_names, has_cols) if h]
    n_out = sum(left_slots) + sum(right_slots)
    outs = pl.pallas_call(
        functools.partial(
            compare_kernel, left_slots, right_slots, tiles, len(left), len(right), has_rows, has_cols
        ),
        out_shape=[jax.ShapeDtypeStruct((1, ROWS), jnp.float32)] * n_out,
        in_specs=[pl.BlockSpec(memory_space=pltpu.VMEM)] * len(args),
        out_specs=[pl.BlockSpec(memory_space=pltpu.VMEM)] * n_out,
        scratch_shapes=[pltpu.VMEM((len(left), ROWS, 128), jnp.float32)],
        compiler_params=pltpu.CompilerParams(vmem_limit_bytes=24 * 1024 * 1024),
        cost_estimate=pl.CostEstimate(
            flops=2 * len(tiles) * ROWS * ROWS * WIDTH,
            bytes_accessed=2 * ROWS * WIDTH * (len(left) + len(right)),
            transcendentals=0,
        ),
    )(*args)
    outs = list(outs)
    new_rows = dict(rows)
    new_rows.update({n: outs.pop(0) for n, s in zip(left_names, left_slots) if s})
    new_cols = dict(cols)
    new_cols.update({n: outs.pop(0) for n, s in zip(right_names, right_slots) if s})
    return new_rows, new_cols


def side(unit, sign):
    route = []
    for i in range(4):
        for j in range(4):
            for k in range(4):
                for c in range(2):
                    route.append((flat(i + sign * (1 - 2 * c), j, k, c), flat(i, j, k, c)))
    return lax.ppermute(unit, AXES, route)


def after(value, *others):
    return lax.optimization_barrier((value, *others))[0]


def on_device(embeddings, cluster, row_index):
    own = pack(embeddings, cluster, row_index)
    p10 = fetch(own, y=1)
    p01 = fetch(own, z=1)
    pmm = fetch(own, y=-1, z=-1)
    near = side(own, 1)
    twin = fetch(own, core=1)
    far = side(after(own, twin), -1)
    near_twin = fetch(near, core=1)
    p10, p01, pmm, near, twin, far, near_twin = lax.optimization_barrier((p10, p01, pmm, near, twin, far, near_twin))
    pm1 = fetch(p01, y=-1)
    pm2 = fetch(pmm, z=-1)
    p21 = fetch(p10, y=1, z=1)
    opposite = side(near, 1)
    far_twin = fetch(far, core=1)
    opposite_twin = fetch(after(opposite, far_twin), core=1)
    left = {"own": own, "twin": twin, "near": near, "near_twin": near_twin, "far": far}
    right = {"own": own, "p10": p10, "p01": p01, "pmm": pmm}
    pairs = [(a, b, "cols" if b == "own" else "both") for b in right for a in left]
    rows, cols = compare(left, right, pairs)
    pm1, pm2, p21, opposite, far_twin, opposite_twin = lax.optimization_barrier(
        (pm1, pm2, p21, opposite, far_twin, opposite_twin)
    )
    p20 = fetch(p10, y=1)
    p02 = fetch(p01, z=1)
    p22 = fetch(pm2, y=-1)
    late = {"far_twin": far_twin, "opposite": opposite, "opposite_twin": opposite_twin}
    pairs = [(a, b, "cols" if b == "own" else "both") for b in right for a in late]
    new = {"pm1": pm1, "pm2": pm2, "p21": p21}
    left = {**left, **late}
    pairs += [(a, b, "both") for b in new for a in left]
    rows, cols = compare(left, {**right, **new}, pairs, rows, cols)
    got = [
        cols["own"],
        give(cols["p10"], y=1),
        give(cols["p01"], z=1),
        give(cols["pmm"], y=-1, z=-1),
        give(cols["pm1"], y=-1, z=1),
        give(cols["pm2"], y=-1, z=-2),
        give(cols["p21"], y=2, z=1),
    ]
    names = ("own", "near", "far", "opposite")
    for_twin = jnp.concatenate([rows["twin"]] + [rows[n + "_twin"] for n in names[1:]], axis=0)
    from_twin = fetch(for_twin, core=1)
    merged = [jnp.maximum(rows[n], from_twin[i : i + 1]) for i, n in enumerate(names)]
    got += [merged[0], side(merged[1], -1), side(merged[2], 1), give(merged[3], x=2)]
    last = {"p20": p20, "p02": p02, "p22": p22}
    _, cols = compare(left, last, [(a, b, "cols") for b in last for a in left])
    got += [give(cols["p20"], y=2), give(cols["p02"], z=2), give(cols["p22"], y=2, z=2)]
    return functools.reduce(jnp.maximum, got).reshape(ROWS)


def solution(mesh):
    fine = Mesh(mesh.devices.reshape(SIZES), AXES)
    return jax.shard_map(
        on_device,
        mesh=fine,
        in_specs=(P(AXES, None), P(AXES), P(AXES)),
        out_specs=P(AXES),
        check_vma=False,
    )
```

```python
import functools

import jax
import jax.numpy as jnp
from jax import lax
from jax.experimental import pallas as pl
from jax.experimental.pallas import tpu as pltpu
from jax.sharding import Mesh, PartitionSpec as P

CL_GROUP = 2
EPSILON = 1e-06
ROWS = 256
WIDTH = 1024
PAD = 16
SIZES = (4, 4, 4, 2)
AXES = ("x", "z", "y", "c")


def flat(x, z, y, c):
    return ((x % 4 * 4 + z % 4) * 4 + y % 4) * 2 + c


def fetch(unit, first, second=None):
    ahead = (first, first if second is None else second)
    route = []
    for i in range(4):
        for j in range(4):
            for k in range(4):
                for c in range(2):
                    x, y, z = ahead[c]
                    route.append((flat(i + x, j + z, k + y, c), flat(i, j, k, c)))
    return lax.ppermute(unit, AXES, route)


def give(values, first, second=None):
    return fetch(values, tuple(-v for v in first), tuple(-v for v in second or first))


def swap(unit):
    return lax.ppermute(unit, AXES, [(i ^ 1, i) for i in range(128)])


def pack_kernel(emb_ref, cluster_ref, index_ref, unit_ref):
    widened = emb_ref[...].astype(jnp.float32)
    scale = lax.rsqrt(jnp.sum(widened * widened, axis=1, keepdims=True) + EPSILON)
    unit_ref[0:ROWS, :] = (widened * scale).astype(jnp.bfloat16)
    cluster = cluster_ref[...]
    index = index_ref[...]
    high = lax.shift_right_logical(index, 8)
    low = index - high * 256
    ids = jnp.concatenate([low, high, cluster, jnp.zeros_like(low)], axis=1).astype(jnp.float32)
    ids = jnp.concatenate([ids, jnp.zeros((PAD - 1, WIDTH), jnp.float32)], axis=0)
    unit_ref[ROWS : ROWS + PAD, :] = ids.astype(jnp.bfloat16)


def pack(embeddings, cluster, row_index):
    return pl.pallas_call(
        pack_kernel,
        out_shape=jax.ShapeDtypeStruct((ROWS + PAD, WIDTH), jnp.bfloat16),
        in_specs=[pl.BlockSpec(memory_space=pltpu.VMEM)] * 3,
        out_specs=pl.BlockSpec(memory_space=pltpu.VMEM),
        cost_estimate=pl.CostEstimate(flops=4 * ROWS * WIDTH, bytes_accessed=4 * ROWS * WIDTH, transcendentals=ROWS),
    )(embeddings, cluster.reshape(1, ROWS), row_index.reshape(1, ROWS))


def ids_of(unit_ref):
    ids = unit_ref[ROWS : ROWS + PAD, :].astype(jnp.float32)[0:1, :]
    order = ids[:, 256:512] * 256.0 + ids[:, 0:256]
    return ids[:, 512:768], order


def compare_kernel(left_slots, right_slots, tiles, n_left, n_right, has_rows, has_cols, *refs):
    left = refs[:n_left]
    right = refs[n_left : n_left + n_right]
    rest = list(refs[n_left + n_right :])
    row_prior = [rest.pop(0) if h else None for h in has_rows]
    col_prior = [rest.pop(0) if h else None for h in has_cols]
    row_outs = [rest.pop(0) if s else None for s in left_slots]
    col_outs = [rest.pop(0) if s else None for s in right_slots]
    row_acc = rest.pop(0)
    low = jnp.float32(-1.0)
    keys = []
    for u in range(n_left):
        cluster, order = ids_of(left[u])
        turned = jnp.concatenate([cluster, order, jnp.zeros((6, ROWS), jnp.float32)], axis=0).T
        keys.append((turned[:, 0:1], turned[:, 1:2]))
    seen = [False] * n_left
    for r in range(n_right):
        right_cluster, right_order = ids_of(right[r])
        col_best = None
        for u, v, rows, cols in tiles:
            if v != r:
                continue
            scores = lax.dot_general(
                left[u][0:ROWS, :], right[r][0:ROWS, :], (((1,), (1,)), ((), ())), preferred_element_type=jnp.float32
            )
            left_cluster, left_order = keys[u]
            scores = jnp.where(left_cluster == right_cluster, scores, low)
            if rows:
                part = jnp.where(right_order < left_order, scores, low)
                part = jnp.maximum(part[:, 0:128], part[:, 128:256])
                row_acc[u] = jnp.maximum(row_acc[u], part) if seen[u] else part
                seen[u] = True
            if cols:
                part = jnp.where(left_order < right_order, scores, low)
                part = jnp.max(part.reshape(ROWS // 8, 8, ROWS), axis=0)
                col_best = part if col_best is None else jnp.maximum(col_best, part)
        if right_slots[r]:
            best = jnp.max(col_best, axis=0, keepdims=True)
            col_outs[r][...] = jnp.maximum(best, col_prior[r][...]) if has_cols[r] else best
    for u in range(n_left):
        if left_slots[u]:
            best = jnp.max(row_acc[u].T, axis=0, keepdims=True)
            row_outs[u][...] = jnp.maximum(best, row_prior[u][...]) if has_rows[u] else best


def compare(left, right, pairs, rows=None, cols=None):
    rows, cols = rows or {}, cols or {}
    left_names, right_names = list(left), list(right)
    tiles = [(left_names.index(a), right_names.index(b), m != "cols", m != "rows") for a, b, m in pairs]
    left_slots = [any(t[0] == i and t[2] for t in tiles) for i in range(len(left))]
    right_slots = [any(t[1] == i and t[3] for t in tiles) for i in range(len(right))]
    has_rows = [n in rows and s for n, s in zip(left_names, left_slots)]
    has_cols = [n in cols and s for n, s in zip(right_names, right_slots)]
    args = [*left.values(), *right.values()]
    args += [rows[n] for n, h in zip(left_names, has_rows) if h]
    args += [cols[n] for n, h in zip(right_names, has_cols) if h]
    n_out = sum(left_slots) + sum(right_slots)
    outs = pl.pallas_call(
        functools.partial(
            compare_kernel, left_slots, right_slots, tiles, len(left), len(right), has_rows, has_cols
        ),
        out_shape=[jax.ShapeDtypeStruct((1, ROWS), jnp.float32)] * n_out,
        in_specs=[pl.BlockSpec(memory_space=pltpu.VMEM)] * len(args),
        out_specs=[pl.BlockSpec(memory_space=pltpu.VMEM)] * n_out,
        scratch_shapes=[pltpu.VMEM((len(left), ROWS, 128), jnp.float32)],
        compiler_params=pltpu.CompilerParams(vmem_limit_bytes=24 * 1024 * 1024),
        cost_estimate=pl.CostEstimate(
            flops=2 * len(tiles) * ROWS * ROWS * WIDTH,
            bytes_accessed=2 * ROWS * WIDTH * (len(left) + len(right)),
            transcendentals=0,
        ),
    )(*args)
    outs = list(outs)
    new_rows = dict(rows)
    new_rows.update({n: outs.pop(0) for n, s in zip(left_names, left_slots) if s})
    new_cols = dict(cols)
    new_cols.update({n: outs.pop(0) for n, s in zip(right_names, right_slots) if s})
    return new_rows, new_cols


def on_device(embeddings, cluster, row_index):
    first_core = lax.axis_index("c") == 0
    own = pack(embeddings, cluster, row_index)
    twin = swap(own)
    corner = fetch(own, (0, -1, -1))
    step_a = fetch(own, (0, 1, 0), (0, 0, 1))
    near_a = fetch(own, (1, 0, 0), (-1, 0, 0))
    step_b = fetch(twin, (0, 1, 0), (0, 0, 1))
    near_b = fetch(twin, (1, 0, 0), (-1, 0, 0))
    two_a = fetch(step_a, (0, 1, 0), (0, 0, 1))
    across = fetch(near_a, (1, 0, 0), (-1, 0, 0))
    two_b = fetch(step_b, (0, 1, 0), (0, 0, 1))
    corner_twin = swap(corner)
    turn_a = fetch(jnp.where(first_core, corner, step_a), (0, 0, -1), (0, -1, 0))
    turn_b = fetch(jnp.where(first_core, corner_twin, step_b), (0, 0, -1), (0, -1, 0))
    far_a = swap(near_a)
    far_b = swap(near_b)
    across_twin = swap(across)
    last_a = fetch(two_a, (0, 0, 1), (0, 2, 0))
    last_b = fetch(two_b, (0, 0, 1), (0, 2, 0))

    left = {"own": own, "twin": twin, "near_a": near_a, "near_b": near_b, "far_a": far_a, "far_b": far_b}
    modes = {"own": "cols", "two_a": "rows", "two_b": "rows"}

    def all_pairs(a, b):
        return [(u, v, modes.get(v, "both")) for v in b for u in a]

    early = {"own": own, "step_a": step_a, "step_b": step_b, "corner": corner}
    rows, cols = compare(left, early, all_pairs(left, early))
    more = {"across": across, "across_twin": across_twin}
    left = {**left, **more}
    twos = {"two_a": two_a, "two_b": two_b}
    rows, cols = compare(left, {**early, **twos}, all_pairs(more, early) + all_pairs(left, twos), rows, cols)
    later = {"turn_a": turn_a, "turn_b": turn_b, "last_a": last_a}
    rows, cols = compare(left, later, all_pairs(left, later), rows, cols)
    final = {"last_b": last_b}
    rows, cols = compare(left, final, all_pairs(left, final), rows, cols)

    def both(name):
        return jnp.concatenate([cols[name + "_a"], cols[name + "_b"]], axis=0)

    step_back = give(both("step"), (0, 1, 0), (0, 0, 1))
    corner_back = give(cols["corner"], (0, -1, -1))
    turn_back = give(both("turn"), (0, -1, -2), (0, -1, 1))
    last_back = give(both("last"), (0, 2, 1), (0, 2, 2))
    partner = swap(jnp.concatenate([rows["twin"], rows["far_a"], rows["far_b"], rows["across_twin"]], axis=0))
    own_rows = jnp.maximum(rows["own"], partner[0:1])
    near_rows = jnp.maximum(jnp.concatenate([rows["near_a"], rows["near_b"]], axis=0), partner[1:3])
    across_rows = jnp.maximum(rows["across"], partner[3:4])
    near_back = give(near_rows, (1, 0, 0), (-1, 0, 0))
    across_back = give(across_rows, (2, 0, 0))
    pairs = functools.reduce(jnp.maximum, [step_back, turn_back, last_back, near_back])
    other = swap(pairs[1:2])
    best = functools.reduce(jnp.maximum, [cols["own"], own_rows, corner_back, across_back, pairs[0:1], other])
    return best.reshape(ROWS)


def solution(mesh):
    fine = Mesh(mesh.devices.reshape(SIZES), AXES)
    return jax.shard_map(
        on_device,
        mesh=fine,
        in_specs=(P(AXES, None), P(AXES), P(AXES)),
        out_specs=P(AXES),
        check_vma=False,
    )
```

```python
import functools

import jax
import jax.numpy as jnp
from jax import lax
from jax.experimental import pallas as pl
from jax.experimental.pallas import tpu as pltpu
from jax.sharding import Mesh, PartitionSpec as P

CL_GROUP = 2
EPSILON = 1e-06
ROWS = 256
WIDTH = 1024
PAD = 16
SIZES = (4, 4, 4, 2)
AXES = ("x", "z", "y", "c")


def flat(x, z, y, c):
    return ((x % 4 * 4 + z % 4) * 4 + y % 4) * 2 + c


def fetch(unit, first, second=None):
    ahead = (first, first if second is None else second)
    route = []
    for i in range(4):
        for j in range(4):
            for k in range(4):
                for c in range(2):
                    x, y, z = ahead[c]
                    route.append((flat(i + x, j + z, k + y, c), flat(i, j, k, c)))
    return lax.ppermute(unit, AXES, route)


def give(values, first, second=None):
    return fetch(values, tuple(-v for v in first), tuple(-v for v in second or first))


def swap(unit):
    return lax.ppermute(unit, AXES, [(i ^ 1, i) for i in range(128)])


def pack_kernel(emb_ref, cluster_ref, index_ref, unit_ref):
    widened = emb_ref[...].astype(jnp.float32)
    scale = lax.rsqrt(jnp.sum(widened * widened, axis=1, keepdims=True) + EPSILON)
    unit_ref[0:ROWS, :] = (widened * scale).astype(jnp.bfloat16)
    cluster = cluster_ref[...]
    index = index_ref[...]
    high = lax.shift_right_logical(index, 8)
    low = index - high * 256
    ids = jnp.concatenate([low, high, cluster, jnp.zeros_like(low)], axis=1).astype(jnp.float32)
    ids = jnp.concatenate([ids, jnp.zeros((PAD - 1, WIDTH), jnp.float32)], axis=0)
    unit_ref[ROWS : ROWS + PAD, :] = ids.astype(jnp.bfloat16)


def pack(embeddings, cluster, row_index):
    return pl.pallas_call(
        pack_kernel,
        out_shape=jax.ShapeDtypeStruct((ROWS + PAD, WIDTH), jnp.bfloat16),
        in_specs=[pl.BlockSpec(memory_space=pltpu.VMEM)] * 3,
        out_specs=pl.BlockSpec(memory_space=pltpu.VMEM),
        cost_estimate=pl.CostEstimate(flops=4 * ROWS * WIDTH, bytes_accessed=4 * ROWS * WIDTH, transcendentals=ROWS),
    )(embeddings, cluster.reshape(1, ROWS), row_index.reshape(1, ROWS))


def ids_of(unit_ref):
    ids = unit_ref[ROWS : ROWS + PAD, :].astype(jnp.float32)[0:1, :]
    order = ids[:, 256:512] * 256.0 + ids[:, 0:256]
    return ids[:, 512:768], order


def compare_kernel(left_slots, right_slots, tiles, n_left, n_right, has_rows, has_cols, *refs):
    left = refs[:n_left]
    right = refs[n_left : n_left + n_right]
    rest = list(refs[n_left + n_right :])
    row_prior = [rest.pop(0) if h else None for h in has_rows]
    col_prior = [rest.pop(0) if h else None for h in has_cols]
    row_outs = [rest.pop(0) if s else None for s in left_slots]
    col_outs = [rest.pop(0) if s else None for s in right_slots]
    row_acc = rest.pop(0)
    low = jnp.float32(-1.0)
    keys = []
    for u in range(n_left):
        cluster, order = ids_of(left[u])
        turned = jnp.concatenate([cluster, order, jnp.zeros((6, ROWS), jnp.float32)], axis=0).T
        keys.append((turned[:, 0:1], turned[:, 1:2]))
    seen = [False] * n_left
    for r in range(n_right):
        right_cluster, right_order = ids_of(right[r])
        col_best = None
        for u, v, rows, cols in tiles:
            if v != r:
                continue
            scores = lax.dot_general(
                left[u][0:ROWS, :], right[r][0:ROWS, :], (((1,), (1,)), ((), ())), preferred_element_type=jnp.float32
            )
            left_cluster, left_order = keys[u]
            scores = jnp.where(left_cluster == right_cluster, scores, low)
            if rows:
                part = jnp.where(right_order < left_order, scores, low)
                part = jnp.maximum(part[:, 0:128], part[:, 128:256])
                row_acc[u] = jnp.maximum(row_acc[u], part) if seen[u] else part
                seen[u] = True
            if cols:
                part = jnp.where(left_order < right_order, scores, low)
                part = jnp.max(part.reshape(ROWS // 8, 8, ROWS), axis=0)
                col_best = part if col_best is None else jnp.maximum(col_best, part)
        if right_slots[r]:
            best = jnp.max(col_best, axis=0, keepdims=True)
            col_outs[r][...] = jnp.maximum(best, col_prior[r][...]) if has_cols[r] else best
    for u in range(n_left):
        if left_slots[u]:
            best = jnp.max(row_acc[u].T, axis=0, keepdims=True)
            row_outs[u][...] = jnp.maximum(best, row_prior[u][...]) if has_rows[u] else best


def compare(left, right, pairs, rows=None, cols=None):
    rows, cols = rows or {}, cols or {}
    left_names, right_names = list(left), list(right)
    tiles = [(left_names.index(a), right_names.index(b), m != "cols", m != "rows") for a, b, m in pairs]
    left_slots = [any(t[0] == i and t[2] for t in tiles) for i in range(len(left))]
    right_slots = [any(t[1] == i and t[3] for t in tiles) for i in range(len(right))]
    has_rows = [n in rows and s for n, s in zip(left_names, left_slots)]
    has_cols = [n in cols and s for n, s in zip(right_names, right_slots)]
    args = [*left.values(), *right.values()]
    args += [rows[n] for n, h in zip(left_names, has_rows) if h]
    args += [cols[n] for n, h in zip(right_names, has_cols) if h]
    n_out = sum(left_slots) + sum(right_slots)
    outs = pl.pallas_call(
        functools.partial(
            compare_kernel, left_slots, right_slots, tiles, len(left), len(right), has_rows, has_cols
        ),
        out_shape=[jax.ShapeDtypeStruct((1, ROWS), jnp.float32)] * n_out,
        in_specs=[pl.BlockSpec(memory_space=pltpu.VMEM)] * len(args),
        out_specs=[pl.BlockSpec(memory_space=pltpu.VMEM)] * n_out,
        scratch_shapes=[pltpu.VMEM((len(left), ROWS, 128), jnp.float32)],
        compiler_params=pltpu.CompilerParams(vmem_limit_bytes=24 * 1024 * 1024),
        cost_estimate=pl.CostEstimate(
            flops=2 * len(tiles) * ROWS * ROWS * WIDTH,
            bytes_accessed=2 * ROWS * WIDTH * (len(left) + len(right)),
            transcendentals=0,
        ),
    )(*args)
    outs = list(outs)
    new_rows = dict(rows)
    new_rows.update({n: outs.pop(0) for n, s in zip(left_names, left_slots) if s})
    new_cols = dict(cols)
    new_cols.update({n: outs.pop(0) for n, s in zip(right_names, right_slots) if s})
    return new_rows, new_cols


def after(value, *others):
    return lax.optimization_barrier((value, *others))[0]


def on_device(embeddings, cluster, row_index):
    own = pack(embeddings, cluster, row_index)
    twin = swap(own)
    step_a = fetch(own, (0, 1, 0), (0, 0, 1))
    step_b = fetch(twin, (0, 1, 0), (0, 0, 1))
    near_a = fetch(after(own, twin), (1, 0, 0), (-1, 0, 0))
    near_b = fetch(twin, (1, 0, 0), (-1, 0, 0))
    two_a = fetch(step_a, (0, 1, 0), (0, 0, 1))
    turn_a = fetch(step_a, (0, 0, -1), (0, -1, 0))
    across = fetch(near_a, (1, 0, 0), (-1, 0, 0))
    far_a = swap(near_a)
    corner = fetch(step_a, (0, 0, 1), (0, 1, 0))
    two_b = fetch(step_b, (0, 1, 0), (0, 0, 1))
    turn_b = fetch(step_b, (0, 0, -1), (0, -1, 0))
    far_b = swap(near_b)
    across_twin = swap(across)

    left = {"own": own, "twin": twin, "near_a": near_a, "near_b": near_b, "far_a": far_a, "far_b": far_b}
    modes = {"own": "cols", "step_a": "both", "step_b": "both", "corner": "both", "last_a": "both", "last_b": "both"}

    def all_pairs(a, b):
        return [(u, v, modes.get(v, "rows")) for v in b for u in a]

    early = {"own": own, "step_a": step_a, "step_b": step_b}
    rows, cols = compare(left, early, all_pairs(left, early))
    last_a = fetch(two_a, (0, 0, -1), (0, -1, 0))
    last_b = fetch(after(two_b, rows["own"]), (0, 0, -1), (0, -1, 0))
    double = fetch(two_a, (0, 0, 2), (0, 2, 0))
    more = {"across": across, "across_twin": across_twin}
    left = {**left, **more}
    second = {"two_a": two_a, "turn_a": turn_a, "corner": corner}
    rows, cols = compare(left, {**early, **second}, all_pairs(more, early) + all_pairs(left, second), rows, cols)
    third = {"two_b": two_b, "turn_b": turn_b, "last_a": last_a, "double": double}
    rows, cols = compare(left, third, all_pairs(left, third), rows, cols)

    def both(name):
        return jnp.concatenate([cols[name + "_a"], cols[name + "_b"]], axis=0)

    step_back = give(both("step"), (0, 1, 0), (0, 0, 1))
    corner_back = give(cols["corner"], (0, 1, 1))
    fourth = {"last_b": after(last_b, step_back, corner_back)}
    rows, cols = compare(left, fourth, all_pairs(left, fourth), rows, cols)
    last_back = give(both("last"), (0, 2, -1), (0, -1, 2))
    partner = swap(jnp.concatenate([rows["twin"], rows["far_a"], rows["far_b"], rows["across_twin"]], axis=0))
    own_rows = jnp.maximum(rows["own"], partner[0:1])
    near_rows = jnp.maximum(jnp.concatenate([rows["near_a"], rows["near_b"]], axis=0), partner[1:3])
    across_rows = jnp.maximum(rows["across"], partner[3:4])
    near_back = give(near_rows, (1, 0, 0), (-1, 0, 0))
    across_back = give(across_rows, (2, 0, 0))
    pairs = functools.reduce(jnp.maximum, [step_back, last_back, near_back])
    other = swap(pairs[1:2])
    best = functools.reduce(jnp.maximum, [cols["own"], own_rows, corner_back, across_back, pairs[0:1], other])
    return best.reshape(ROWS)


def solution(mesh):
    fine = Mesh(mesh.devices.reshape(SIZES), AXES)
    return jax.shard_map(
        on_device,
        mesh=fine,
        in_specs=(P(AXES, None), P(AXES), P(AXES)),
        out_specs=P(AXES),
        check_vma=False,
    )
```

```python
import functools

import jax
import jax.numpy as jnp
from jax import lax
from jax.experimental import pallas as pl
from jax.experimental.pallas import tpu as pltpu
from jax.sharding import Mesh, PartitionSpec as P

CL_GROUP = 2
EPSILON = 1e-06
ROWS = 256
WIDTH = 1024
PAD = 16
SIZES = (4, 4, 4, 2)
AXES = ("x", "z", "y", "c")


def flat(x, z, y, c):
    return ((x % 4 * 4 + z % 4) * 4 + y % 4) * 2 + c


def fetch(unit, first, second=None):
    ahead = (first, first if second is None else second)
    route = []
    for i in range(4):
        for j in range(4):
            for k in range(4):
                for c in range(2):
                    x, y, z = ahead[c]
                    route.append((flat(i + x, j + z, k + y, c), flat(i, j, k, c)))
    return lax.ppermute(unit, AXES, route)


def give(values, first, second=None):
    return fetch(values, tuple(-v for v in first), tuple(-v for v in second or first))


def swap(unit):
    return lax.ppermute(unit, AXES, [(i ^ 1, i) for i in range(128)])


def pack_kernel(emb_ref, cluster_ref, index_ref, unit_ref):
    widened = emb_ref[...].astype(jnp.float32)
    scale = lax.rsqrt(jnp.sum(widened * widened, axis=1, keepdims=True) + EPSILON)
    unit_ref[0:ROWS, :] = (widened * scale).astype(jnp.bfloat16)
    cluster = cluster_ref[...]
    index = index_ref[...]
    high = lax.shift_right_logical(index, 8)
    low = index - high * 256
    ids = jnp.concatenate([low, high, cluster, jnp.zeros_like(low)], axis=1).astype(jnp.float32)
    ids = jnp.concatenate([ids, jnp.zeros((PAD - 1, WIDTH), jnp.float32)], axis=0)
    unit_ref[ROWS : ROWS + PAD, :] = ids.astype(jnp.bfloat16)


def pack(embeddings, cluster, row_index):
    return pl.pallas_call(
        pack_kernel,
        out_shape=jax.ShapeDtypeStruct((ROWS + PAD, WIDTH), jnp.bfloat16),
        in_specs=[pl.BlockSpec(memory_space=pltpu.VMEM)] * 3,
        out_specs=pl.BlockSpec(memory_space=pltpu.VMEM),
        cost_estimate=pl.CostEstimate(flops=4 * ROWS * WIDTH, bytes_accessed=4 * ROWS * WIDTH, transcendentals=ROWS),
    )(embeddings, cluster.reshape(1, ROWS), row_index.reshape(1, ROWS))


def ids_of(unit_ref):
    ids = unit_ref[ROWS : ROWS + PAD, :].astype(jnp.float32)[0:1, :]
    order = ids[:, 256:512] * 256.0 + ids[:, 0:256]
    return ids[:, 512:768], order


def compare_kernel(left_slots, right_slots, tiles, n_left, n_right, has_rows, has_cols, *refs):
    left = refs[:n_left]
    right = refs[n_left : n_left + n_right]
    rest = list(refs[n_left + n_right :])
    row_prior = [rest.pop(0) if h else None for h in has_rows]
    col_prior = [rest.pop(0) if h else None for h in has_cols]
    row_outs = [rest.pop(0) if s else None for s in left_slots]
    col_outs = [rest.pop(0) if s else None for s in right_slots]
    row_acc = rest.pop(0)
    low = jnp.float32(-1.0)
    keys = []
    for u in range(n_left):
        cluster, order = ids_of(left[u])
        turned = jnp.concatenate([cluster, order, jnp.zeros((6, ROWS), jnp.float32)], axis=0).T
        keys.append((turned[:, 0:1], turned[:, 1:2]))
    seen = [False] * n_left
    for r in range(n_right):
        right_cluster, right_order = ids_of(right[r])
        col_best = None
        for u, v, rows, cols in tiles:
            if v != r:
                continue
            scores = lax.dot_general(
                left[u][0:ROWS, :], right[r][0:ROWS, :], (((1,), (1,)), ((), ())), preferred_element_type=jnp.float32
            )
            left_cluster, left_order = keys[u]
            scores = jnp.where(left_cluster == right_cluster, scores, low)
            if rows:
                part = jnp.where(right_order < left_order, scores, low)
                part = jnp.maximum(part[:, 0:128], part[:, 128:256])
                row_acc[u] = jnp.maximum(row_acc[u], part) if seen[u] else part
                seen[u] = True
            if cols:
                part = jnp.where(left_order < right_order, scores, low)
                part = jnp.max(part.reshape(ROWS // 8, 8, ROWS), axis=0)
                col_best = part if col_best is None else jnp.maximum(col_best, part)
        if right_slots[r]:
            best = jnp.max(col_best, axis=0, keepdims=True)
            col_outs[r][...] = jnp.maximum(best, col_prior[r][...]) if has_cols[r] else best
    for u in range(n_left):
        if left_slots[u]:
            best = jnp.max(row_acc[u].T, axis=0, keepdims=True)
            row_outs[u][...] = jnp.maximum(best, row_prior[u][...]) if has_rows[u] else best


def compare(left, right, pairs, rows=None, cols=None):
    rows, cols = rows or {}, cols or {}
    left_names, right_names = list(left), list(right)
    tiles = [(left_names.index(a), right_names.index(b), m != "cols", m != "rows") for a, b, m in pairs]
    left_slots = [any(t[0] == i and t[2] for t in tiles) for i in range(len(left))]
    right_slots = [any(t[1] == i and t[3] for t in tiles) for i in range(len(right))]
    has_rows = [n in rows and s for n, s in zip(left_names, left_slots)]
    has_cols = [n in cols and s for n, s in zip(right_names, right_slots)]
    args = [*left.values(), *right.values()]
    args += [rows[n] for n, h in zip(left_names, has_rows) if h]
    args += [cols[n] for n, h in zip(right_names, has_cols) if h]
    n_out = sum(left_slots) + sum(right_slots)
    outs = pl.pallas_call(
        functools.partial(
            compare_kernel, left_slots, right_slots, tiles, len(left), len(right), has_rows, has_cols
        ),
        out_shape=[jax.ShapeDtypeStruct((1, ROWS), jnp.float32)] * n_out,
        in_specs=[pl.BlockSpec(memory_space=pltpu.VMEM)] * len(args),
        out_specs=[pl.BlockSpec(memory_space=pltpu.VMEM)] * n_out,
        scratch_shapes=[pltpu.VMEM((len(left), ROWS, 128), jnp.float32)],
        compiler_params=pltpu.CompilerParams(vmem_limit_bytes=24 * 1024 * 1024),
        cost_estimate=pl.CostEstimate(
            flops=2 * len(tiles) * ROWS * ROWS * WIDTH,
            bytes_accessed=2 * ROWS * WIDTH * (len(left) + len(right)),
            transcendentals=0,
        ),
    )(*args)
    outs = list(outs)
    new_rows = dict(rows)
    new_rows.update({n: outs.pop(0) for n, s in zip(left_names, left_slots) if s})
    new_cols = dict(cols)
    new_cols.update({n: outs.pop(0) for n, s in zip(right_names, right_slots) if s})
    return new_rows, new_cols


def after(value, *others):
    return lax.optimization_barrier((value, *others))[0]


def on_device(embeddings, cluster, row_index):
    own = pack(embeddings, cluster, row_index)
    twin = swap(own)
    step_a = fetch(own, (0, 1, 0), (0, 0, 1))
    near_a = fetch(own, (1, 0, 0), (-1, 0, 0))
    step_b = fetch(twin, (0, 1, 0), (0, 0, 1))
    near_b = fetch(twin, (1, 0, 0), (-1, 0, 0))
    two_a = fetch(step_a, (0, 1, 0), (0, 0, 1))
    turn_a = fetch(step_a, (0, 0, -1), (0, -1, 0))
    across = fetch(after(near_a, step_a), (1, 0, 0), (-1, 0, 0))
    two_b = fetch(step_b, (0, 1, 0), (0, 0, 1))
    far_a = swap(after(near_a, step_b))
    far_b = swap(after(near_b, far_a, turn_a))
    turn_b = fetch(after(step_b, turn_a), (0, 0, -1), (0, -1, 0))
    across_twin = swap(after(across, two_a, turn_a))
    last_a = fetch(two_a, (0, 0, -1), (0, -1, 0))

    left = {"own": own, "twin": twin, "near_a": near_a, "near_b": near_b, "far_a": far_a, "far_b": far_b}
    modes = {"own": "cols", "step_a": "both", "step_b": "both", "corner": "both", "last_a": "both", "last_b": "both"}

    def all_pairs(a, b):
        return [(u, v, modes.get(v, "rows")) for v in b for u in a]

    early = {"own": own, "step_a": step_a, "step_b": step_b, "turn_a": turn_a}
    rows, cols = compare(left, early, all_pairs(left, early))
    two_b = after(two_b, rows["own"])
    corner = fetch(after(step_a, two_b), (0, 0, 1), (0, 1, 0))
    double = fetch(after(two_a, rows["own"]), (0, 0, 2), (0, 2, 0))
    last_b = fetch(two_b, (0, 0, -1), (0, -1, 0))
    more = {"across": across, "across_twin": across_twin}
    left = {**left, **more}
    second = {"two_a": two_a}
    rows, cols = compare(left, {**early, **second}, all_pairs(more, early) + all_pairs(left, second), rows, cols)
    third = {"two_b": two_b, "turn_b": turn_b, "last_a": last_a, "double": double}
    rows, cols = compare(left, third, all_pairs(left, third), rows, cols)

    def both(name):
        return jnp.concatenate([cols[name + "_a"], cols[name + "_b"]], axis=0)

    step_back = give(both("step"), (0, 1, 0), (0, 0, 1))
    fourth = {"corner": after(corner, step_back), "last_b": last_b}
    rows, cols = compare(left, fourth, all_pairs(left, fourth), rows, cols)
    corner_back = give(cols["corner"], (0, 1, 1))
    last_back = give(both("last"), (0, 2, -1), (0, -1, 2))
    partner = swap(jnp.concatenate([rows["twin"], rows["far_a"], rows["far_b"], rows["across_twin"]], axis=0))
    own_rows = jnp.maximum(rows["own"], partner[0:1])
    near_rows = jnp.maximum(jnp.concatenate([rows["near_a"], rows["near_b"]], axis=0), partner[1:3])
    across_rows = jnp.maximum(rows["across"], partner[3:4])
    near_back = give(near_rows, (1, 0, 0), (-1, 0, 0))
    across_back = give(across_rows, (2, 0, 0))
    pairs = functools.reduce(jnp.maximum, [step_back, last_back, near_back])
    other = swap(pairs[1:2])
    best = functools.reduce(jnp.maximum, [cols["own"], own_rows, corner_back, across_back, pairs[0:1], other])
    return best.reshape(ROWS)


def solution(mesh):
    fine = Mesh(mesh.devices.reshape(SIZES), AXES)
    return jax.shard_map(
        on_device,
        mesh=fine,
        in_specs=(P(AXES, None), P(AXES), P(AXES)),
        out_specs=P(AXES),
        check_vma=False,
    )
```

```python
import functools

import jax
import jax.numpy as jnp
from jax import lax
from jax.experimental import pallas as pl
from jax.experimental.pallas import tpu as pltpu
from jax.sharding import Mesh, PartitionSpec as P

CL_GROUP = 2
EPSILON = 1e-06
ROWS = 256
WIDTH = 1024
PAD = 16
SIZES = (4, 4, 4, 2)
AXES = ("x", "z", "y", "c")


def flat(x, z, y, c):
    return ((x % 4 * 4 + z % 4) * 4 + y % 4) * 2 + c


def fetch(unit, first, second=None):
    ahead = (first, first if second is None else second)
    route = []
    for i in range(4):
        for j in range(4):
            for k in range(4):
                for c in range(2):
                    x, y, z = ahead[c]
                    route.append((flat(i + x, j + z, k + y, c), flat(i, j, k, c)))
    return lax.ppermute(unit, AXES, route)


def give(values, first, second=None):
    return fetch(values, tuple(-v for v in first), tuple(-v for v in second or first))


def swap(unit):
    return lax.ppermute(unit, AXES, [(i ^ 1, i) for i in range(128)])


def pack_kernel(emb_ref, cluster_ref, index_ref, unit_ref):
    widened = emb_ref[...].astype(jnp.float32)
    scale = lax.rsqrt(jnp.sum(widened * widened, axis=1, keepdims=True) + EPSILON)
    unit_ref[0:ROWS, :] = (widened * scale).astype(jnp.bfloat16)
    cluster = cluster_ref[...]
    index = index_ref[...]
    high = lax.shift_right_logical(index, 8)
    low = index - high * 256
    ids = jnp.concatenate([low, high, cluster, jnp.zeros_like(low)], axis=1).astype(jnp.float32)
    ids = jnp.concatenate([ids, jnp.zeros((PAD - 1, WIDTH), jnp.float32)], axis=0)
    unit_ref[ROWS : ROWS + PAD, :] = ids.astype(jnp.bfloat16)


def pack(embeddings, cluster, row_index):
    return pl.pallas_call(
        pack_kernel,
        out_shape=jax.ShapeDtypeStruct((ROWS + PAD, WIDTH), jnp.bfloat16),
        in_specs=[pl.BlockSpec(memory_space=pltpu.VMEM)] * 3,
        out_specs=pl.BlockSpec(memory_space=pltpu.VMEM),
        cost_estimate=pl.CostEstimate(flops=4 * ROWS * WIDTH, bytes_accessed=4 * ROWS * WIDTH, transcendentals=ROWS),
    )(embeddings, cluster.reshape(1, ROWS), row_index.reshape(1, ROWS))


def ids_of(unit_ref):
    ids = unit_ref[ROWS : ROWS + PAD, :].astype(jnp.float32)[0:1, :]
    order = ids[:, 256:512] * 256.0 + ids[:, 0:256]
    return ids[:, 512:768], order


def compare_kernel(left_slots, right_slots, tiles, n_left, n_right, has_rows, has_cols, *refs):
    left = refs[:n_left]
    right = refs[n_left : n_left + n_right]
    rest = list(refs[n_left + n_right :])
    row_prior = [rest.pop(0) if h else None for h in has_rows]
    col_prior = [rest.pop(0) if h else None for h in has_cols]
    row_outs = [rest.pop(0) if s else None for s in left_slots]
    col_outs = [rest.pop(0) if s else None for s in right_slots]
    row_acc = rest.pop(0)
    low = jnp.float32(-1.0)
    keys = []
    for u in range(n_left):
        cluster, order = ids_of(left[u])
        turned = jnp.concatenate([cluster, order, jnp.zeros((6, ROWS), jnp.float32)], axis=0).T
        keys.append((turned[:, 0:1], turned[:, 1:2]))
    seen = [False] * n_left
    for r in range(n_right):
        right_cluster, right_order = ids_of(right[r])
        col_best = None
        for u, v, rows, cols in tiles:
            if v != r:
                continue
            scores = lax.dot_general(
                left[u][0:ROWS, :], right[r][0:ROWS, :], (((1,), (1,)), ((), ())), preferred_element_type=jnp.float32
            )
            left_cluster, left_order = keys[u]
            scores = jnp.where(left_cluster == right_cluster, scores, low)
            if rows:
                part = jnp.where(right_order < left_order, scores, low)
                part = jnp.maximum(part[:, 0:128], part[:, 128:256])
                row_acc[u] = jnp.maximum(row_acc[u], part) if seen[u] else part
                seen[u] = True
            if cols:
                part = jnp.where(left_order < right_order, scores, low)
                part = jnp.max(part.reshape(ROWS // 8, 8, ROWS), axis=0)
                col_best = part if col_best is None else jnp.maximum(col_best, part)
        if right_slots[r]:
            best = jnp.max(col_best, axis=0, keepdims=True)
            col_outs[r][...] = jnp.maximum(best, col_prior[r][...]) if has_cols[r] else best
    for u in range(n_left):
        if left_slots[u]:
            best = jnp.max(row_acc[u].T, axis=0, keepdims=True)
            row_outs[u][...] = jnp.maximum(best, row_prior[u][...]) if has_rows[u] else best


def compare(left, right, pairs, rows=None, cols=None):
    rows, cols = rows or {}, cols or {}
    left_names, right_names = list(left), list(right)
    tiles = [(left_names.index(a), right_names.index(b), m != "cols", m != "rows") for a, b, m in pairs]
    left_slots = [any(t[0] == i and t[2] for t in tiles) for i in range(len(left))]
    right_slots = [any(t[1] == i and t[3] for t in tiles) for i in range(len(right))]
    has_rows = [n in rows and s for n, s in zip(left_names, left_slots)]
    has_cols = [n in cols and s for n, s in zip(right_names, right_slots)]
    args = [*left.values(), *right.values()]
    args += [rows[n] for n, h in zip(left_names, has_rows) if h]
    args += [cols[n] for n, h in zip(right_names, has_cols) if h]
    n_out = sum(left_slots) + sum(right_slots)
    outs = pl.pallas_call(
        functools.partial(
            compare_kernel, left_slots, right_slots, tiles, len(left), len(right), has_rows, has_cols
        ),
        out_shape=[jax.ShapeDtypeStruct((1, ROWS), jnp.float32)] * n_out,
        in_specs=[pl.BlockSpec(memory_space=pltpu.VMEM)] * len(args),
        out_specs=[pl.BlockSpec(memory_space=pltpu.VMEM)] * n_out,
        scratch_shapes=[pltpu.VMEM((len(left), ROWS, 128), jnp.float32)],
        compiler_params=pltpu.CompilerParams(vmem_limit_bytes=24 * 1024 * 1024),
        cost_estimate=pl.CostEstimate(
            flops=2 * len(tiles) * ROWS * ROWS * WIDTH // 16, bytes_accessed=ROWS, transcendentals=0
        ),
    )(*args)
    outs = list(outs)
    new_rows = dict(rows)
    new_rows.update({n: outs.pop(0) for n, s in zip(left_names, left_slots) if s})
    new_cols = dict(cols)
    new_cols.update({n: outs.pop(0) for n, s in zip(right_names, right_slots) if s})
    return new_rows, new_cols


def after(value, *others):
    return lax.optimization_barrier((value, *others))[0]


def on_device(embeddings, cluster, row_index):
    own = pack(embeddings, cluster, row_index)
    twin = swap(own)
    step_a = fetch(own, (0, 1, 0), (0, 0, 1))
    near_a = fetch(own, (1, 0, 0), (-1, 0, 0))
    step_b = fetch(twin, (0, 1, 0), (0, 0, 1))
    near_b = fetch(twin, (1, 0, 0), (-1, 0, 0))
    two_a = fetch(step_a, (0, 1, 0), (0, 0, 1))
    turn_a = fetch(step_a, (0, 0, -1), (0, -1, 0))
    across = fetch(after(near_a, step_a), (1, 0, 0), (-1, 0, 0))
    two_b = fetch(step_b, (0, 1, 0), (0, 0, 1))
    far_a = swap(after(near_a, two_a))
    far_b = swap(after(near_b, far_a, turn_a))
    turn_b = fetch(after(step_b, turn_a), (0, 0, -1), (0, -1, 0))
    across_twin = swap(after(across, two_a, turn_a))
    last_a = fetch(two_a, (0, 0, -1), (0, -1, 0))

    left = {"own": own, "twin": twin, "near_a": near_a, "near_b": near_b, "far_a": far_a, "far_b": far_b}
    modes = {"own": "cols", "step_a": "both", "step_b": "both", "corner": "both", "last_a": "both", "last_b": "both"}

    def all_pairs(a, b):
        return [(u, v, modes.get(v, "rows")) for v in b for u in a]

    early = {"own": own, "step_a": step_a, "step_b": step_b, "turn_a": turn_a}
    rows, cols = compare(left, early, all_pairs(left, early))
    two_b = after(two_b, rows["own"])
    corner = fetch(after(step_a, two_b, turn_b), (0, 0, 1), (0, 1, 0))
    double = fetch(after(two_a, last_a), (0, 0, 2), (0, 2, 0))
    last_b = fetch(two_b, (0, 0, -1), (0, -1, 0))
    more = {"across": across, "across_twin": across_twin}
    left = {**left, **more}
    second = {"two_a": two_a}
    rows, cols = compare(left, {**early, **second}, all_pairs(more, early) + all_pairs(left, second), rows, cols)
    third = {"two_b": two_b, "turn_b": turn_b, "last_a": last_a, "double": double}
    rows, cols = compare(left, third, all_pairs(left, third), rows, cols)

    def both(name):
        return jnp.concatenate([cols[name + "_a"], cols[name + "_b"]], axis=0)

    step_back = give(both("step"), (0, 1, 0), (0, 0, 1))
    fourth = {"corner": after(corner, step_back), "last_b": last_b}
    rows, cols = compare(left, fourth, all_pairs(left, fourth), rows, cols)
    corner_back = give(cols["corner"], (0, 1, 1))
    last_back = give(both("last"), (0, 2, -1), (0, -1, 2))
    partner = swap(jnp.concatenate([rows["twin"], rows["far_a"], rows["far_b"], rows["across_twin"]], axis=0))
    own_rows = jnp.maximum(rows["own"], partner[0:1])
    near_rows = jnp.maximum(jnp.concatenate([rows["near_a"], rows["near_b"]], axis=0), partner[1:3])
    across_rows = jnp.maximum(rows["across"], partner[3:4])
    near_back = give(near_rows, (1, 0, 0), (-1, 0, 0))
    across_back = give(across_rows, (2, 0, 0))
    pairs = functools.reduce(jnp.maximum, [step_back, last_back, near_back])
    other = swap(pairs[1:2])
    best = functools.reduce(jnp.maximum, [cols["own"], own_rows, corner_back, across_back, pairs[0:1], other])
    return best.reshape(ROWS)


def solution(mesh):
    fine = Mesh(mesh.devices.reshape(SIZES), AXES)
    return jax.shard_map(
        on_device,
        mesh=fine,
        in_specs=(P(AXES, None), P(AXES), P(AXES)),
        out_specs=P(AXES),
        check_vma=False,
    )
```

```python
import functools

import jax
import jax.numpy as jnp
from jax import lax
from jax.experimental import pallas as pl
from jax.experimental.pallas import tpu as pltpu
from jax.sharding import Mesh, PartitionSpec as P

CL_GROUP = 2
EPSILON = 1e-06
ROWS = 256
WIDTH = 1024
PAD = 16
SIZES = (4, 4, 4, 2)
AXES = ("x", "z", "y", "c")


def flat(x, z, y, c):
    return ((x % 4 * 4 + z % 4) * 4 + y % 4) * 2 + c


def fetch(unit, first, second=None):
    ahead = (first, first if second is None else second)
    route = []
    for i in range(4):
        for j in range(4):
            for k in range(4):
                for c in range(2):
                    x, y, z = ahead[c]
                    route.append((flat(i + x, j + z, k + y, c), flat(i, j, k, c)))
    return lax.ppermute(unit, AXES, route)


def give(values, first, second=None):
    return fetch(values, tuple(-v for v in first), tuple(-v for v in second or first))


def swap(unit):
    return lax.ppermute(unit, AXES, [(i ^ 1, i) for i in range(128)])


def pack_kernel(emb_ref, cluster_ref, index_ref, unit_ref):
    widened = emb_ref[...].astype(jnp.float32)
    scale = lax.rsqrt(jnp.sum(widened * widened, axis=1, keepdims=True) + EPSILON)
    unit_ref[0:ROWS, :] = (widened * scale).astype(jnp.bfloat16)
    cluster = cluster_ref[...]
    index = index_ref[...]
    high = lax.shift_right_logical(index, 8)
    low = index - high * 256
    ids = jnp.concatenate([low, high, cluster, jnp.zeros_like(low)], axis=1).astype(jnp.float32)
    ids = jnp.concatenate([ids, jnp.zeros((PAD - 1, WIDTH), jnp.float32)], axis=0)
    unit_ref[ROWS : ROWS + PAD, :] = ids.astype(jnp.bfloat16)


def pack(embeddings, cluster, row_index):
    return pl.pallas_call(
        pack_kernel,
        out_shape=jax.ShapeDtypeStruct((ROWS + PAD, WIDTH), jnp.bfloat16),
        in_specs=[pl.BlockSpec(memory_space=pltpu.VMEM)] * 3,
        out_specs=pl.BlockSpec(memory_space=pltpu.VMEM),
        cost_estimate=pl.CostEstimate(flops=4 * ROWS * WIDTH, bytes_accessed=4 * ROWS * WIDTH, transcendentals=ROWS),
    )(embeddings, cluster.reshape(1, ROWS), row_index.reshape(1, ROWS))


def ids_of(unit_ref):
    ids = unit_ref[ROWS : ROWS + PAD, :].astype(jnp.float32)[0:1, :]
    order = ids[:, 256:512] * 256.0 + ids[:, 0:256]
    return ids[:, 512:768], order


def compare_kernel(left_slots, right_slots, tiles, n_left, n_right, has_rows, has_cols, *refs):
    left = refs[:n_left]
    right = refs[n_left : n_left + n_right]
    rest = list(refs[n_left + n_right :])
    row_prior = [rest.pop(0) if h else None for h in has_rows]
    col_prior = [rest.pop(0) if h else None for h in has_cols]
    row_outs = [rest.pop(0) if s else None for s in left_slots]
    col_outs = [rest.pop(0) if s else None for s in right_slots]
    row_acc = rest.pop(0)
    low = jnp.float32(-1.0)
    keys = []
    for u in range(n_left):
        cluster, order = ids_of(left[u])
        turned = jnp.concatenate([cluster, order, jnp.zeros((6, ROWS), jnp.float32)], axis=0).T
        keys.append((turned[:, 0:1], turned[:, 1:2]))
    seen = [False] * n_left
    for r in range(n_right):
        right_cluster, right_order = ids_of(right[r])
        col_best = None
        for u, v, rows, cols in tiles:
            if v != r:
                continue
            scores = lax.dot_general(
                left[u][0:ROWS, :], right[r][0:ROWS, :], (((1,), (1,)), ((), ())), preferred_element_type=jnp.float32
            )
            left_cluster, left_order = keys[u]
            scores = jnp.where(left_cluster == right_cluster, scores, low)
            if rows:
                part = jnp.where(right_order < left_order, scores, low)
                part = jnp.maximum(part[:, 0:128], part[:, 128:256])
                row_acc[u] = jnp.maximum(row_acc[u], part) if seen[u] else part
                seen[u] = True
            if cols:
                part = jnp.where(left_order < right_order, scores, low)
                part = jnp.max(part.reshape(ROWS // 8, 8, ROWS), axis=0)
                col_best = part if col_best is None else jnp.maximum(col_best, part)
        if right_slots[r]:
            best = jnp.max(col_best, axis=0, keepdims=True)
            col_outs[r][...] = jnp.maximum(best, col_prior[r][...]) if has_cols[r] else best
    for u in range(n_left):
        if left_slots[u]:
            best = jnp.max(row_acc[u].T, axis=0, keepdims=True)
            row_outs[u][...] = jnp.maximum(best, row_prior[u][...]) if has_rows[u] else best


def compare(left, right, pairs, rows=None, cols=None):
    rows, cols = rows or {}, cols or {}
    left_names, right_names = list(left), list(right)
    tiles = [(left_names.index(a), right_names.index(b), m != "cols", m != "rows") for a, b, m in pairs]
    left_slots = [any(t[0] == i and t[2] for t in tiles) for i in range(len(left))]
    right_slots = [any(t[1] == i and t[3] for t in tiles) for i in range(len(right))]
    has_rows = [n in rows and s for n, s in zip(left_names, left_slots)]
    has_cols = [n in cols and s for n, s in zip(right_names, right_slots)]
    args = [*left.values(), *right.values()]
    args += [rows[n] for n, h in zip(left_names, has_rows) if h]
    args += [cols[n] for n, h in zip(right_names, has_cols) if h]
    n_out = sum(left_slots) + sum(right_slots)
    outs = pl.pallas_call(
        functools.partial(
            compare_kernel, left_slots, right_slots, tiles, len(left), len(right), has_rows, has_cols
        ),
        out_shape=[jax.ShapeDtypeStruct((1, ROWS), jnp.float32)] * n_out,
        in_specs=[pl.BlockSpec(memory_space=pltpu.VMEM)] * len(args),
        out_specs=[pl.BlockSpec(memory_space=pltpu.VMEM)] * n_out,
        scratch_shapes=[pltpu.VMEM((len(left), ROWS, 128), jnp.float32)],
        compiler_params=pltpu.CompilerParams(vmem_limit_bytes=24 * 1024 * 1024),
        cost_estimate=pl.CostEstimate(
            flops=2 * len(tiles) * ROWS * ROWS * WIDTH // 16, bytes_accessed=ROWS, transcendentals=0
        ),
    )(*args)
    outs = list(outs)
    new_rows = dict(rows)
    new_rows.update({n: outs.pop(0) for n, s in zip(left_names, left_slots) if s})
    new_cols = dict(cols)
    new_cols.update({n: outs.pop(0) for n, s in zip(right_names, right_slots) if s})
    return new_rows, new_cols


def after(value, *others):
    return lax.optimization_barrier((value, *others))[0]


def on_device(embeddings, cluster, row_index):
    own = pack(embeddings, cluster, row_index)
    twin = swap(own)
    step_a = fetch(own, (0, 1, 0), (0, 0, 1))
    near_a = fetch(own, (1, 0, 0), (-1, 0, 0))
    step_b = fetch(twin, (0, 1, 0), (0, 0, 1))
    near_b = fetch(twin, (1, 0, 0), (-1, 0, 0))
    two_a = fetch(step_a, (0, 1, 0), (0, 0, 1))
    turn_a = fetch(step_a, (0, 0, -1), (0, -1, 0))
    across = fetch(after(near_a, step_a), (1, 0, 0), (-1, 0, 0))
    two_b = fetch(step_b, (0, 1, 0), (0, 0, 1))
    far_a = swap(after(near_a, step_b))
    far_b = swap(after(near_b, far_a, turn_a))
    turn_b = fetch(after(step_b, turn_a), (0, 0, -1), (0, -1, 0))
    across_twin = swap(after(across, two_a, turn_a))
    last_a = fetch(two_a, (0, 0, -1), (0, -1, 0))

    left = {"own": own, "twin": twin, "near_a": near_a, "near_b": near_b, "far_a": far_a, "far_b": far_b}
    modes = {"own": "cols", "step_a": "both", "step_b": "both", "corner": "both", "last_a": "both", "last_b": "both"}

    def all_pairs(a, b):
        return [(u, v, modes.get(v, "rows")) for v in b for u in a]

    early = {"own": own, "step_a": step_a, "step_b": step_b, "turn_a": turn_a}
    rows, cols = compare(left, early, all_pairs(left, early))
    two_b = after(two_b, rows["own"])
    corner = fetch(after(step_a, two_b, turn_b), (0, 0, 1), (0, 1, 0))
    double = fetch(after(two_a, last_a), (0, 0, 2), (0, 2, 0))
    last_b = fetch(two_b, (0, 0, -1), (0, -1, 0))
    more = {"across": across, "across_twin": across_twin}
    left = {**left, **more}
    second = {"two_a": two_a}
    rows, cols = compare(left, {**early, **second}, all_pairs(more, early) + all_pairs(left, second), rows, cols)
    third = {"two_b": two_b, "turn_b": turn_b, "last_a": last_a, "double": double}
    rows, cols = compare(left, third, all_pairs(left, third), rows, cols)

    def both(name):
        return jnp.concatenate([cols[name + "_a"], cols[name + "_b"]], axis=0)

    step_back = give(both("step"), (0, 1, 0), (0, 0, 1))
    fourth = {"corner": after(corner, step_back), "last_b": last_b}
    rows, cols = compare(left, fourth, all_pairs(left, fourth), rows, cols)
    corner_back = give(cols["corner"], (0, 1, 1))
    last_back = give(both("last"), (0, 2, -1), (0, -1, 2))
    partner = swap(jnp.concatenate([rows["twin"], rows["far_a"], rows["far_b"], rows["across_twin"]], axis=0))
    own_rows = jnp.maximum(rows["own"], partner[0:1])
    near_rows = jnp.maximum(jnp.concatenate([rows["near_a"], rows["near_b"]], axis=0), partner[1:3])
    across_rows = jnp.maximum(rows["across"], partner[3:4])
    near_back = give(near_rows, (1, 0, 0), (-1, 0, 0))
    across_back = give(across_rows, (2, 0, 0))
    pairs = functools.reduce(jnp.maximum, [step_back, last_back, near_back])
    other = swap(pairs[1:2])
    best = functools.reduce(jnp.maximum, [cols["own"], own_rows, corner_back, across_back, pairs[0:1], other])
    return best.reshape(ROWS)


def solution(mesh):
    fine = Mesh(mesh.devices.reshape(SIZES), AXES)
    return jax.shard_map(
        on_device,
        mesh=fine,
        in_specs=(P(AXES, None), P(AXES), P(AXES)),
        out_specs=P(AXES),
        check_vma=False,
    )
```

```python
import functools

import jax
import jax.numpy as jnp
from jax import lax
from jax.experimental import pallas as pl
from jax.experimental.pallas import tpu as pltpu
from jax.sharding import Mesh, PartitionSpec as P

CL_GROUP = 2
EPSILON = 1e-06
ROWS = 256
WIDTH = 1024
PAD = 16
SIZES = (4, 4, 4, 2)
AXES = ("x", "z", "y", "c")


def flat(x, z, y, c):
    return ((x % 4 * 4 + z % 4) * 4 + y % 4) * 2 + c


def fetch(unit, first, second=None):
    ahead = (first, first if second is None else second)
    route = []
    for i in range(4):
        for j in range(4):
            for k in range(4):
                for c in range(2):
                    x, y, z = ahead[c]
                    route.append((flat(i + x, j + z, k + y, c), flat(i, j, k, c)))
    return lax.ppermute(unit, AXES, route)


def give(values, first, second=None):
    return fetch(values, tuple(-v for v in first), tuple(-v for v in second or first))


def swap(unit):
    return lax.ppermute(unit, AXES, [(i ^ 1, i) for i in range(128)])


def pack_kernel(emb_ref, cluster_ref, index_ref, unit_ref):
    widened = emb_ref[...].astype(jnp.float32)
    scale = lax.rsqrt(jnp.sum(widened * widened, axis=1, keepdims=True) + EPSILON)
    unit_ref[0:ROWS, :] = (widened * scale).astype(jnp.bfloat16)
    cluster = cluster_ref[...]
    index = index_ref[...]
    high = lax.shift_right_logical(index, 8)
    low = index - high * 256
    ids = jnp.concatenate([low, high, cluster, jnp.zeros_like(low)], axis=1).astype(jnp.float32)
    ids = jnp.concatenate([ids, jnp.zeros((PAD - 1, WIDTH), jnp.float32)], axis=0)
    unit_ref[ROWS : ROWS + PAD, :] = ids.astype(jnp.bfloat16)


def pack(embeddings, cluster, row_index):
    return pl.pallas_call(
        pack_kernel,
        out_shape=jax.ShapeDtypeStruct((ROWS + PAD, WIDTH), jnp.bfloat16),
        in_specs=[pl.BlockSpec(memory_space=pltpu.VMEM)] * 3,
        out_specs=pl.BlockSpec(memory_space=pltpu.VMEM),
        cost_estimate=pl.CostEstimate(flops=4 * ROWS * WIDTH, bytes_accessed=4 * ROWS * WIDTH, transcendentals=ROWS),
    )(embeddings, cluster.reshape(1, ROWS), row_index.reshape(1, ROWS))


def ids_of(unit_ref):
    ids = unit_ref[ROWS : ROWS + PAD, :].astype(jnp.float32)[0:1, :]
    order = ids[:, 256:512] * 256.0 + ids[:, 0:256]
    return ids[:, 512:768], order


def compare_kernel(left_slots, right_slots, tiles, n_left, n_right, has_rows, has_cols, *refs):
    left = refs[:n_left]
    right = refs[n_left : n_left + n_right]
    rest = list(refs[n_left + n_right :])
    row_prior = [rest.pop(0) if h else None for h in has_rows]
    col_prior = [rest.pop(0) if h else None for h in has_cols]
    row_outs = [rest.pop(0) if s else None for s in left_slots]
    col_outs = [rest.pop(0) if s else None for s in right_slots]
    row_acc = rest.pop(0)
    low = jnp.float32(-1.0)
    keys = []
    for u in range(n_left):
        cluster, order = ids_of(left[u])
        turned = jnp.concatenate([cluster, order, jnp.zeros((6, ROWS), jnp.float32)], axis=0).T
        keys.append((turned[:, 0:1], turned[:, 1:2]))
    seen = [False] * n_left
    for r in range(n_right):
        right_cluster, right_order = ids_of(right[r])
        col_best = None
        for u, v, rows, cols in tiles:
            if v != r:
                continue
            scores = lax.dot_general(
                left[u][0:ROWS, :], right[r][0:ROWS, :], (((1,), (1,)), ((), ())), preferred_element_type=jnp.float32
            )
            left_cluster, left_order = keys[u]
            scores = jnp.where(left_cluster == right_cluster, scores, low)
            if rows:
                part = jnp.where(right_order < left_order, scores, low)
                part = jnp.maximum(part[:, 0:128], part[:, 128:256])
                row_acc[u] = jnp.maximum(row_acc[u], part) if seen[u] else part
                seen[u] = True
            if cols:
                part = jnp.where(left_order < right_order, scores, low)
                part = jnp.max(part.reshape(ROWS // 8, 8, ROWS), axis=0)
                col_best = part if col_best is None else jnp.maximum(col_best, part)
        if right_slots[r]:
            best = jnp.max(col_best, axis=0, keepdims=True)
            col_outs[r][...] = jnp.maximum(best, col_prior[r][...]) if has_cols[r] else best
    for u in range(n_left):
        if left_slots[u]:
            best = jnp.max(row_acc[u].T, axis=0, keepdims=True)
            row_outs[u][...] = jnp.maximum(best, row_prior[u][...]) if has_rows[u] else best


def compare(left, right, pairs, rows=None, cols=None):
    rows, cols = rows or {}, cols or {}
    left_names, right_names = list(left), list(right)
    tiles = [(left_names.index(a), right_names.index(b), m != "cols", m != "rows") for a, b, m in pairs]
    left_slots = [any(t[0] == i and t[2] for t in tiles) for i in range(len(left))]
    right_slots = [any(t[1] == i and t[3] for t in tiles) for i in range(len(right))]
    has_rows = [n in rows and s for n, s in zip(left_names, left_slots)]
    has_cols = [n in cols and s for n, s in zip(right_names, right_slots)]
    args = [*left.values(), *right.values()]
    args += [rows[n] for n, h in zip(left_names, has_rows) if h]
    args += [cols[n] for n, h in zip(right_names, has_cols) if h]
    n_out = sum(left_slots) + sum(right_slots)
    outs = pl.pallas_call(
        functools.partial(
            compare_kernel, left_slots, right_slots, tiles, len(left), len(right), has_rows, has_cols
        ),
        out_shape=[jax.ShapeDtypeStruct((1, ROWS), jnp.float32)] * n_out,
        in_specs=[pl.BlockSpec(memory_space=pltpu.VMEM)] * len(args),
        out_specs=[pl.BlockSpec(memory_space=pltpu.VMEM)] * n_out,
        scratch_shapes=[pltpu.VMEM((len(left), ROWS, 128), jnp.float32)],
        compiler_params=pltpu.CompilerParams(vmem_limit_bytes=24 * 1024 * 1024),
        cost_estimate=pl.CostEstimate(
            flops=2 * len(tiles) * ROWS * ROWS * WIDTH // 16, bytes_accessed=ROWS, transcendentals=0
        ),
    )(*args)
    outs = list(outs)
    new_rows = dict(rows)
    new_rows.update({n: outs.pop(0) for n, s in zip(left_names, left_slots) if s})
    new_cols = dict(cols)
    new_cols.update({n: outs.pop(0) for n, s in zip(right_names, right_slots) if s})
    return new_rows, new_cols


def after(value, *others):
    return lax.optimization_barrier((value, *others))[0]


def on_device(embeddings, cluster, row_index):
    own = pack(embeddings, cluster, row_index)
    step_a = fetch(own, (0, 1, 0), (0, 0, 1))
    twin = swap(own)
    near_a = fetch(own, (1, 0, 0), (-1, 0, 0))
    step_b = fetch(twin, (0, 1, 0), (0, 0, 1))
    near_b = fetch(twin, (1, 0, 0), (-1, 0, 0))
    two_a = fetch(step_a, (0, 1, 0), (0, 0, 1))
    turn_a = fetch(step_a, (0, 0, -1), (0, 1, 0))
    two_b = fetch(step_b, (0, 1, 0), (0, 0, 1))
    far_a = swap(after(near_a, step_b))
    across = fetch(after(near_a, step_a), (1, 0, 0), (-1, 0, 0))
    far_b = swap(after(near_b, far_a, turn_a))
    turn_b = fetch(after(step_b, turn_a), (0, 0, -1), (0, 1, 0))
    last_a = fetch(two_a, (0, 0, -1), (0, -1, 0))
    across_twin = swap(after(across, two_a, turn_a))

    left = {"own": own, "twin": twin, "near_a": near_a, "near_b": near_b, "far_a": far_a, "far_b": far_b}
    modes = {"own": "cols", "two_a": "rows", "two_b": "rows", "double": "rows"}

    def all_pairs(a, b):
        return [(u, v, modes.get(v, "both")) for v in b for u in a]

    early = {"own": own, "step_a": step_a, "step_b": step_b, "turn_a": turn_a}
    rows, cols = compare(left, early, all_pairs(left, early))
    double = fetch(after(two_a, last_a), (0, 0, 2), (0, 2, 0))
    last_b = fetch(after(two_b, rows["own"]), (0, 0, -1), (0, -1, 0))
    more = {"across": across, "across_twin": across_twin}
    left = {**left, **more}
    second = {"two_a": two_a}
    rows, cols = compare(left, {**early, **second}, all_pairs(more, early) + all_pairs(left, second), rows, cols)

    def both(name):
        return jnp.concatenate([cols[name + "_a"], cols[name + "_b"]], axis=0)

    step_back = give(both("step"), (0, 1, 0), (0, 0, 1))
    third = {"two_b": two_b, "turn_b": turn_b, "last_a": last_a, "double": double}
    rows, cols = compare(left, third, all_pairs(left, third), rows, cols)
    fourth = {"last_b": after(last_b, step_back)}
    rows, cols = compare(left, fourth, all_pairs(left, fourth), rows, cols)
    turn_back = give(both("turn"), (0, 1, -1), (0, 1, 1))
    last_back = give(both("last"), (0, 2, -1), (0, -1, 2))
    partner = swap(jnp.concatenate([rows["twin"], rows["far_a"], rows["far_b"], rows["across_twin"]], axis=0))
    own_rows = jnp.maximum(rows["own"], partner[0:1])
    near_rows = jnp.maximum(jnp.concatenate([rows["near_a"], rows["near_b"]], axis=0), partner[1:3])
    across_rows = jnp.maximum(rows["across"], partner[3:4])
    near_back = give(near_rows, (1, 0, 0), (-1, 0, 0))
    across_back = give(across_rows, (2, 0, 0))
    pairs = functools.reduce(jnp.maximum, [step_back, turn_back, last_back, near_back])
    other = swap(pairs[1:2])
    best = functools.reduce(jnp.maximum, [cols["own"], own_rows, across_back, pairs[0:1], other])
    return best.reshape(ROWS)


def solution(mesh):
    fine = Mesh(mesh.devices.reshape(SIZES), AXES)
    return jax.shard_map(
        on_device,
        mesh=fine,
        in_specs=(P(AXES, None), P(AXES), P(AXES)),
        out_specs=P(AXES),
        check_vma=False,
    )
```

```python
import functools

import jax
import jax.numpy as jnp
from jax import lax
from jax.experimental import pallas as pl
from jax.experimental.pallas import tpu as pltpu
from jax.sharding import Mesh, PartitionSpec as P

CL_GROUP = 2
EPSILON = 1e-06
ROWS = 256
WIDTH = 1024
PAD = 16
SIZES = (4, 4, 4, 2)
AXES = ("x", "z", "y", "c")


def flat(x, z, y, c):
    return ((x % 4 * 4 + z % 4) * 4 + y % 4) * 2 + c


def fetch(unit, first, second=None):
    ahead = (first, first if second is None else second)
    route = []
    for i in range(4):
        for j in range(4):
            for k in range(4):
                for c in range(2):
                    x, y, z = ahead[c]
                    route.append((flat(i + x, j + z, k + y, c), flat(i, j, k, c)))
    return lax.ppermute(unit, AXES, route)


def give(values, first, second=None):
    return fetch(values, tuple(-v for v in first), tuple(-v for v in second or first))


def swap(unit):
    return lax.ppermute(unit, AXES, [(i ^ 1, i) for i in range(128)])


def pack_kernel(emb_ref, cluster_ref, index_ref, unit_ref):
    widened = emb_ref[...].astype(jnp.float32)
    scale = lax.rsqrt(jnp.sum(widened * widened, axis=1, keepdims=True) + EPSILON)
    unit_ref[0:ROWS, :] = (widened * scale).astype(jnp.bfloat16)
    cluster = cluster_ref[...]
    index = index_ref[...]
    high = lax.shift_right_logical(index, 8)
    low = index - high * 256
    ids = jnp.concatenate([low, high, cluster, jnp.zeros_like(low)], axis=1).astype(jnp.float32)
    ids = jnp.concatenate([ids, jnp.zeros((PAD - 1, WIDTH), jnp.float32)], axis=0)
    unit_ref[ROWS : ROWS + PAD, :] = ids.astype(jnp.bfloat16)


def pack(embeddings, cluster, row_index):
    return pl.pallas_call(
        pack_kernel,
        out_shape=pltpu.VMEM((ROWS + PAD, WIDTH), jnp.bfloat16),
        in_specs=[pl.BlockSpec(memory_space=pltpu.VMEM)] * 3,
        out_specs=pl.BlockSpec(memory_space=pltpu.VMEM),
        cost_estimate=pl.CostEstimate(flops=4 * ROWS * WIDTH, bytes_accessed=4 * ROWS * WIDTH, transcendentals=ROWS),
    )(embeddings, cluster.reshape(1, ROWS), row_index.reshape(1, ROWS))


def ids_of(unit_ref):
    ids = unit_ref[ROWS : ROWS + PAD, :].astype(jnp.float32)[0:1, :]
    order = ids[:, 256:512] * 256.0 + ids[:, 0:256]
    return ids[:, 512:768], order


def compare_kernel(left_slots, right_slots, tiles, n_left, n_right, has_rows, has_cols, *refs):
    left = refs[:n_left]
    right = refs[n_left : n_left + n_right]
    rest = list(refs[n_left + n_right :])
    row_prior = [rest.pop(0) if h else None for h in has_rows]
    col_prior = [rest.pop(0) if h else None for h in has_cols]
    row_outs = [rest.pop(0) if s else None for s in left_slots]
    col_outs = [rest.pop(0) if s else None for s in right_slots]
    row_acc = rest.pop(0)
    low = jnp.float32(-1.0)
    keys = []
    for u in range(n_left):
        cluster, order = ids_of(left[u])
        turned = jnp.concatenate([cluster, order, jnp.zeros((6, ROWS), jnp.float32)], axis=0).T
        keys.append((turned[:, 0:1], turned[:, 1:2]))
    seen = [False] * n_left
    for r in range(n_right):
        right_cluster, right_order = ids_of(right[r])
        col_best = None
        for u, v, rows, cols in tiles:
            if v != r:
                continue
            scores = lax.dot_general(
                left[u][0:ROWS, :], right[r][0:ROWS, :], (((1,), (1,)), ((), ())), preferred_element_type=jnp.float32
            )
            left_cluster, left_order = keys[u]
            scores = jnp.where(left_cluster == right_cluster, scores, low)
            if rows:
                part = jnp.where(right_order < left_order, scores, low)
                part = jnp.maximum(part[:, 0:128], part[:, 128:256])
                row_acc[u] = jnp.maximum(row_acc[u], part) if seen[u] else part
                seen[u] = True
            if cols:
                part = jnp.where(left_order < right_order, scores, low)
                part = jnp.max(part.reshape(ROWS // 8, 8, ROWS), axis=0)
                col_best = part if col_best is None else jnp.maximum(col_best, part)
        if right_slots[r]:
            best = jnp.max(col_best, axis=0, keepdims=True)
            col_outs[r][...] = jnp.maximum(best, col_prior[r][...]) if has_cols[r] else best
    for u in range(n_left):
        if left_slots[u]:
            best = jnp.max(row_acc[u].T, axis=0, keepdims=True)
            row_outs[u][...] = jnp.maximum(best, row_prior[u][...]) if has_rows[u] else best


def compare(left, right, pairs, rows=None, cols=None):
    rows, cols = rows or {}, cols or {}
    left_names, right_names = list(left), list(right)
    tiles = [(left_names.index(a), right_names.index(b), m != "cols", m != "rows") for a, b, m in pairs]
    left_slots = [any(t[0] == i and t[2] for t in tiles) for i in range(len(left))]
    right_slots = [any(t[1] == i and t[3] for t in tiles) for i in range(len(right))]
    has_rows = [n in rows and s for n, s in zip(left_names, left_slots)]
    has_cols = [n in cols and s for n, s in zip(right_names, right_slots)]
    args = [*left.values(), *right.values()]
    args += [rows[n] for n, h in zip(left_names, has_rows) if h]
    args += [cols[n] for n, h in zip(right_names, has_cols) if h]
    n_out = sum(left_slots) + sum(right_slots)
    outs = pl.pallas_call(
        functools.partial(
            compare_kernel, left_slots, right_slots, tiles, len(left), len(right), has_rows, has_cols
        ),
        out_shape=[jax.ShapeDtypeStruct((1, ROWS), jnp.float32)] * n_out,
        in_specs=[pl.BlockSpec(memory_space=pltpu.VMEM)] * len(args),
        out_specs=[pl.BlockSpec(memory_space=pltpu.VMEM)] * n_out,
        scratch_shapes=[pltpu.VMEM((len(left), ROWS, 128), jnp.float32)],
        compiler_params=pltpu.CompilerParams(vmem_limit_bytes=24 * 1024 * 1024),
        cost_estimate=pl.CostEstimate(
            flops=2 * len(tiles) * ROWS * ROWS * WIDTH // 16, bytes_accessed=ROWS, transcendentals=0
        ),
    )(*args)
    outs = list(outs)
    new_rows = dict(rows)
    new_rows.update({n: outs.pop(0) for n, s in zip(left_names, left_slots) if s})
    new_cols = dict(cols)
    new_cols.update({n: outs.pop(0) for n, s in zip(right_names, right_slots) if s})
    return new_rows, new_cols


def after(value, *others):
    return lax.optimization_barrier((value, *others))[0]


def on_device(embeddings, cluster, row_index):
    modes = {"own": "cols"}
    modes.update({n: "rows" for n in ("two_a", "two_b", "turn_a", "turn_b", "double")})

    def all_pairs(a, b):
        return [(u, v, modes.get(v, "both")) for v in b for u in a]

    own = pack(embeddings, cluster, row_index)
    twin = swap(own)
    step_a = fetch(own, (0, 1, 0), (0, 0, 1))
    near_a = fetch(own, (1, 0, 0), (-1, 0, 0))
    step_b = fetch(twin, (0, 1, 0), (0, 0, 1))
    near_b = fetch(twin, (1, 0, 0), (-1, 0, 0))
    two_a = fetch(step_a, (0, 1, 0), (0, 0, 1))
    turn_a = fetch(step_a, (0, 0, -1), (0, -1, 0))
    two_b = fetch(step_b, (0, 1, 0), (0, 0, 1))
    far_a = swap(after(near_a, step_b))
    right = {"own": own, "step_a": step_a, "step_b": step_b}
    left = {"own": own, "twin": twin, "near_a": near_a}
    rows, cols = compare(left, right, all_pairs(left, right))
    first = rows["own"]
    across = fetch(after(near_a, step_a), (1, 0, 0), (-1, 0, 0))
    far_b = swap(after(near_b, far_a, turn_a, first))
    turn_b = fetch(after(step_b, turn_a), (0, 0, -1), (0, -1, 0))
    last_a = fetch(two_a, (0, 0, -1), (0, -1, 0))
    rest = {"near_b": near_b, "far_a": far_a, "far_b": far_b}
    left = {**left, **rest}
    more = {"turn_a": turn_a}
    rows, cols = compare(left, {**right, **more}, all_pairs(rest, right) + all_pairs(left, more), rows, cols)
    second = rows["own"]
    across_twin = swap(after(across, two_a, turn_a))
    corner = fetch(after(step_a, two_b, turn_b), (0, 0, 1), (0, 1, 0))
    double = fetch(last_a, (0, 0, -1), (0, -1, 0))

    last_b = fetch(two_b, (0, 0, -1), (0, -1, 0))
    right = {**right, **more}
    rest = {"across": across, "across_twin": across_twin}
    left = {**left, **rest}
    more = {"two_a": two_a}
    rows, cols = compare(left, {**right, **more}, all_pairs(rest, right) + all_pairs(left, more), rows, cols)

    def both(name):
        return jnp.concatenate([cols[name + "_a"], cols[name + "_b"]], axis=0)

    step_back = give(both("step"), (0, 1, 0), (0, 0, 1))

    more = {"two_b": two_b, "turn_b": turn_b, "last_a": last_a, "double": double}
    rows, cols = compare(left, more, all_pairs(left, more), rows, cols)

    more = {"last_b": after(last_b, step_back), "corner": corner}
    rows, cols = compare(left, more, all_pairs(left, more), rows, cols)
    corner_back = give(cols["corner"], (0, 1, 1))
    last_back = give(both("last"), (0, 2, -1), (0, -1, 2))
    partner = swap(jnp.concatenate([rows["twin"], rows["far_a"], rows["far_b"], rows["across_twin"]], axis=0))
    own_rows = jnp.maximum(rows["own"], partner[0:1])
    near_rows = jnp.maximum(jnp.concatenate([rows["near_a"], rows["near_b"]], axis=0), partner[1:3])
    across_rows = jnp.maximum(rows["across"], partner[3:4])
    near_back = give(near_rows, (1, 0, 0), (-1, 0, 0))
    across_back = give(across_rows, (2, 0, 0))
    pairs = functools.reduce(jnp.maximum, [step_back, last_back, near_back])
    other = swap(pairs[1:2])
    best = functools.reduce(jnp.maximum, [cols["own"], own_rows, corner_back, across_back, pairs[0:1], other])
    return best.reshape(ROWS)


def solution(mesh):
    fine = Mesh(mesh.devices.reshape(SIZES), AXES)
    return jax.shard_map(
        on_device,
        mesh=fine,
        in_specs=(P(AXES, None), P(AXES), P(AXES)),
        out_specs=P(AXES),
        check_vma=False,
    )
```

```python
import functools

import jax
import jax.numpy as jnp
from jax import lax
from jax.experimental import pallas as pl
from jax.experimental.pallas import tpu as pltpu
from jax.sharding import Mesh, PartitionSpec as P

CL_GROUP = 2
EPSILON = 1e-06
ROWS = 256
WIDTH = 1024
PAD = 16
SIZES = (4, 4, 4, 2)
AXES = ("x", "z", "y", "c")


def flat(x, z, y, c):
    return ((x % 4 * 4 + z % 4) * 4 + y % 4) * 2 + c


def fetch(unit, first, second=None):
    ahead = (first, first if second is None else second)
    route = []
    for i in range(4):
        for j in range(4):
            for k in range(4):
                for c in range(2):
                    x, y, z = ahead[c]
                    route.append((flat(i + x, j + z, k + y, c), flat(i, j, k, c)))
    return lax.ppermute(unit, AXES, route)


def give(values, first, second=None):
    return fetch(values, tuple(-v for v in first), tuple(-v for v in second or first))


def swap(unit):
    return lax.ppermute(unit, AXES, [(i ^ 1, i) for i in range(128)])


def pack_kernel(emb_ref, cluster_ref, index_ref, unit_ref):
    widened = emb_ref[...].astype(jnp.float32)
    scale = lax.rsqrt(jnp.sum(widened * widened, axis=1, keepdims=True) + EPSILON)
    unit_ref[0:ROWS, :] = (widened * scale).astype(jnp.bfloat16)
    cluster = cluster_ref[...]
    index = index_ref[...]
    high = lax.shift_right_logical(index, 8)
    low = index - high * 256
    ids = jnp.concatenate([low, high, cluster, jnp.zeros_like(low)], axis=1).astype(jnp.float32)
    ids = jnp.concatenate([ids, jnp.zeros((PAD - 1, WIDTH), jnp.float32)], axis=0)
    unit_ref[ROWS : ROWS + PAD, :] = ids.astype(jnp.bfloat16)


def pack(embeddings, cluster, row_index):
    return pl.pallas_call(
        pack_kernel,
        out_shape=pltpu.VMEM((ROWS + PAD, WIDTH), jnp.bfloat16),
        in_specs=[pl.BlockSpec(memory_space=pltpu.VMEM)] * 3,
        out_specs=pl.BlockSpec(memory_space=pltpu.VMEM),
        cost_estimate=pl.CostEstimate(flops=4 * ROWS * WIDTH, bytes_accessed=4 * ROWS * WIDTH, transcendentals=ROWS),
    )(embeddings, cluster.reshape(1, ROWS), row_index.reshape(1, ROWS))


def ids_of(unit_ref):
    ids = unit_ref[ROWS : ROWS + PAD, :].astype(jnp.float32)[0:1, :]
    order = ids[:, 256:512] * 256.0 + ids[:, 0:256]
    return ids[:, 512:768], order


def compare_kernel(left_slots, right_slots, tiles, n_left, n_right, has_rows, has_cols, *refs):
    left = refs[:n_left]
    right = refs[n_left : n_left + n_right]
    rest = list(refs[n_left + n_right :])
    row_prior = [rest.pop(0) if h else None for h in has_rows]
    col_prior = [rest.pop(0) if h else None for h in has_cols]
    row_outs = [rest.pop(0) if s else None for s in left_slots]
    col_outs = [rest.pop(0) if s else None for s in right_slots]
    row_acc = rest.pop(0)
    low = jnp.float32(-1.0)
    keys = []
    for u in range(n_left):
        cluster, order = ids_of(left[u])
        turned = jnp.concatenate([cluster, order, jnp.zeros((6, ROWS), jnp.float32)], axis=0).T
        keys.append((turned[:, 0:1], turned[:, 1:2]))
    seen = [False] * n_left
    for r in range(n_right):
        right_cluster, right_order = ids_of(right[r])
        col_best = None
        for u, v, rows, cols in tiles:
            if v != r:
                continue
            scores = lax.dot_general(
                left[u][0:ROWS, :], right[r][0:ROWS, :], (((1,), (1,)), ((), ())), preferred_element_type=jnp.float32
            )
            left_cluster, left_order = keys[u]
            scores = jnp.where(left_cluster == right_cluster, scores, low)
            if rows:
                part = jnp.where(right_order < left_order, scores, low)
                part = jnp.maximum(part[:, 0:128], part[:, 128:256])
                row_acc[u] = jnp.maximum(row_acc[u], part) if seen[u] else part
                seen[u] = True
            if cols:
                part = jnp.where(left_order < right_order, scores, low)
                part = jnp.max(part.reshape(ROWS // 8, 8, ROWS), axis=0)
                col_best = part if col_best is None else jnp.maximum(col_best, part)
        if right_slots[r]:
            best = jnp.max(col_best, axis=0, keepdims=True)
            col_outs[r][...] = jnp.maximum(best, col_prior[r][...]) if has_cols[r] else best
    for u in range(n_left):
        if left_slots[u]:
            best = jnp.max(row_acc[u].T, axis=0, keepdims=True)
            row_outs[u][...] = jnp.maximum(best, row_prior[u][...]) if has_rows[u] else best


def compare(left, right, pairs, rows=None, cols=None):
    rows, cols = rows or {}, cols or {}
    left_names, right_names = list(left), list(right)
    tiles = [(left_names.index(a), right_names.index(b), m != "cols", m != "rows") for a, b, m in pairs]
    left_slots = [any(t[0] == i and t[2] for t in tiles) for i in range(len(left))]
    right_slots = [any(t[1] == i and t[3] for t in tiles) for i in range(len(right))]
    has_rows = [n in rows and s for n, s in zip(left_names, left_slots)]
    has_cols = [n in cols and s for n, s in zip(right_names, right_slots)]
    args = [*left.values(), *right.values()]
    args += [rows[n] for n, h in zip(left_names, has_rows) if h]
    args += [cols[n] for n, h in zip(right_names, has_cols) if h]
    n_out = sum(left_slots) + sum(right_slots)
    outs = pl.pallas_call(
        functools.partial(
            compare_kernel, left_slots, right_slots, tiles, len(left), len(right), has_rows, has_cols
        ),
        out_shape=[jax.ShapeDtypeStruct((1, ROWS), jnp.float32)] * n_out,
        in_specs=[pl.BlockSpec(memory_space=pltpu.VMEM)] * len(args),
        out_specs=[pl.BlockSpec(memory_space=pltpu.VMEM)] * n_out,
        scratch_shapes=[pltpu.VMEM((len(left), ROWS, 128), jnp.float32)],
        compiler_params=pltpu.CompilerParams(vmem_limit_bytes=24 * 1024 * 1024),
        cost_estimate=pl.CostEstimate(
            flops=2 * len(tiles) * ROWS * ROWS * WIDTH // 4, bytes_accessed=ROWS, transcendentals=0
        ),
    )(*args)
    outs = list(outs)
    new_rows = dict(rows)
    new_rows.update({n: outs.pop(0) for n, s in zip(left_names, left_slots) if s})
    new_cols = dict(cols)
    new_cols.update({n: outs.pop(0) for n, s in zip(right_names, right_slots) if s})
    return new_rows, new_cols


def after(value, *others):
    return lax.optimization_barrier((value, *others))[0]


def on_device(embeddings, cluster, row_index):
    modes = {"own": "cols"}
    modes.update({n: "rows" for n in ("two_a", "two_b", "turn_a", "turn_b", "double")})

    def all_pairs(a, b):
        return [(u, v, modes.get(v, "both")) for v in b for u in a]

    own = pack(embeddings, cluster, row_index)
    twin = swap(own)
    step_a = fetch(own, (0, 1, 0), (0, 0, 1))
    near_a = fetch(own, (1, 0, 0), (-1, 0, 0))
    step_b = fetch(twin, (0, 1, 0), (0, 0, 1))
    near_b = fetch(twin, (1, 0, 0), (-1, 0, 0))
    two_a = fetch(step_a, (0, 1, 0), (0, 0, 1))
    turn_a = fetch(step_a, (0, 0, -1), (0, -1, 0))
    two_b = fetch(step_b, (0, 1, 0), (0, 0, 1))
    far_a = swap(after(near_a, step_b))
    right = {"own": own, "step_a": step_a, "step_b": step_b, "turn_a": turn_a}
    left = {"own": own, "twin": twin, "near_a": near_a, "near_b": near_b}
    rows, cols = compare(left, right, all_pairs(left, right))
    first = rows["own"]
    across = fetch(after(near_a, step_a), (1, 0, 0), (-1, 0, 0))
    far_b = swap(after(near_b, far_a, turn_a, first))
    turn_b = fetch(step_b, (0, 0, -1), (0, -1, 0))
    last_a = fetch(two_a, (0, 0, -1), (0, -1, 0))
    rest = {"far_a": far_a, "far_b": far_b}
    left = {**left, **rest}
    more = {"two_a": two_a}
    rows, cols = compare(left, {**right, **more}, all_pairs(rest, right) + all_pairs(left, more), rows, cols)
    second = rows["own"]
    across_twin = swap(after(across, two_a, turn_a))
    corner = fetch(after(step_a, two_b, second), (0, 0, 1), (0, 1, 0))
    double = fetch(last_a, (0, 0, -1), (0, -1, 0))

    last_b = fetch(two_b, (0, 0, -1), (0, -1, 0))
    right = {**right, **more}
    rest = {"across": across, "across_twin": across_twin}
    left = {**left, **rest}
    more = {"two_b": two_b}
    rows, cols = compare(left, {**right, **more}, all_pairs(rest, right) + all_pairs(left, more), rows, cols)

    def both(name):
        return jnp.concatenate([cols[name + "_a"], cols[name + "_b"]], axis=0)

    step_back = give(both("step"), (0, 1, 0), (0, 0, 1))
    more = {"turn_b": turn_b, "last_a": last_a, "double": double}
    rows, cols = compare(left, more, all_pairs(left, more), rows, cols)
    more = {"last_b": after(last_b, step_back), "corner": corner}
    rows, cols = compare(left, more, all_pairs(left, more), rows, cols)
    corner_back = give(cols["corner"], (0, 1, 1))
    last_back = give(both("last"), (0, 2, -1), (0, -1, 2))
    partner = swap(jnp.concatenate([rows["twin"], rows["far_a"], rows["far_b"], rows["across_twin"]], axis=0))
    own_rows = jnp.maximum(rows["own"], partner[0:1])
    near_rows = jnp.maximum(jnp.concatenate([rows["near_a"], rows["near_b"]], axis=0), partner[1:3])
    across_rows = jnp.maximum(rows["across"], partner[3:4])
    near_back = give(near_rows, (1, 0, 0), (-1, 0, 0))
    across_back = give(across_rows, (2, 0, 0))
    pairs = functools.reduce(jnp.maximum, [step_back, last_back, near_back])
    other = swap(pairs[1:2])
    best = functools.reduce(jnp.maximum, [cols["own"], own_rows, corner_back, across_back, pairs[0:1], other])
    return best.reshape(ROWS)


def solution(mesh):
    fine = Mesh(mesh.devices.reshape(SIZES), AXES)
    return jax.shard_map(
        on_device,
        mesh=fine,
        in_specs=(P(AXES, None), P(AXES), P(AXES)),
        out_specs=P(AXES),
        check_vma=False,
    )
```

```python
import functools

import jax
import jax.numpy as jnp
from jax import lax
from jax.experimental import pallas as pl
from jax.experimental.pallas import tpu as pltpu
from jax.sharding import Mesh, PartitionSpec as P

CL_GROUP = 2
EPSILON = 1e-06
ROWS = 256
WIDTH = 1024
PAD = 16
SIZES = (4, 4, 4, 2)
AXES = ("x", "z", "y", "c")


def flat(x, z, y, c):
    return ((x % 4 * 4 + z % 4) * 4 + y % 4) * 2 + c


def fetch(unit, first, second=None):
    ahead = (first, first if second is None else second)
    route = []
    for i in range(4):
        for j in range(4):
            for k in range(4):
                for c in range(2):
                    x, y, z = ahead[c]
                    route.append((flat(i + x, j + z, k + y, c), flat(i, j, k, c)))
    return lax.ppermute(unit, AXES, route)


def give(values, first, second=None):
    return fetch(values, tuple(-v for v in first), tuple(-v for v in second or first))


def swap(unit):
    return lax.ppermute(unit, AXES, [(i ^ 1, i) for i in range(128)])


def pack_kernel(emb_ref, cluster_ref, index_ref, unit_ref):
    widened = emb_ref[...].astype(jnp.float32)
    scale = lax.rsqrt(jnp.sum(widened * widened, axis=1, keepdims=True) + EPSILON)
    unit_ref[0:ROWS, :] = (widened * scale).astype(jnp.bfloat16)
    cluster = cluster_ref[...]
    index = index_ref[...]
    high = lax.shift_right_logical(index, 8)
    low = index - high * 256
    ids = jnp.concatenate([low, high, cluster, jnp.zeros_like(low)], axis=1).astype(jnp.float32)
    ids = jnp.concatenate([ids, jnp.zeros((PAD - 1, WIDTH), jnp.float32)], axis=0)
    unit_ref[ROWS : ROWS + PAD, :] = ids.astype(jnp.bfloat16)


def pack(embeddings, cluster, row_index):
    return pl.pallas_call(
        pack_kernel,
        out_shape=pltpu.VMEM((ROWS + PAD, WIDTH), jnp.bfloat16),
        in_specs=[pl.BlockSpec(memory_space=pltpu.VMEM)] * 3,
        out_specs=pl.BlockSpec(memory_space=pltpu.VMEM),
        cost_estimate=pl.CostEstimate(flops=4 * ROWS * WIDTH, bytes_accessed=4 * ROWS * WIDTH, transcendentals=ROWS),
    )(embeddings, cluster.reshape(1, ROWS), row_index.reshape(1, ROWS))


def ids_of(unit_ref):
    ids = unit_ref[ROWS : ROWS + PAD, :].astype(jnp.float32)[0:1, :]
    order = ids[:, 256:512] * 256.0 + ids[:, 0:256]
    return ids[:, 512:768], order


def compare_kernel(left_slots, right_slots, tiles, n_left, n_right, has_rows, has_cols, *refs):
    left = refs[:n_left]
    right = refs[n_left : n_left + n_right]
    rest = list(refs[n_left + n_right :])
    row_prior = [rest.pop(0) if h else None for h in has_rows]
    col_prior = [rest.pop(0) if h else None for h in has_cols]
    row_outs = [rest.pop(0) if s else None for s in left_slots]
    col_outs = [rest.pop(0) if s else None for s in right_slots]
    row_acc = rest.pop(0)
    low = jnp.float32(-1.0)
    keys = []
    for u in range(n_left):
        cluster, order = ids_of(left[u])
        turned = jnp.concatenate([cluster, order, jnp.zeros((6, ROWS), jnp.float32)], axis=0).T
        keys.append((turned[:, 0:1], turned[:, 1:2]))
    seen = [False] * n_left
    for r in range(n_right):
        right_cluster, right_order = ids_of(right[r])
        col_best = None
        for u, v, rows, cols in tiles:
            if v != r:
                continue
            scores = lax.dot_general(
                left[u][0:ROWS, :], right[r][0:ROWS, :], (((1,), (1,)), ((), ())), preferred_element_type=jnp.float32
            )
            left_cluster, left_order = keys[u]
            scores = jnp.where(left_cluster == right_cluster, scores, low)
            if rows:
                part = jnp.where(right_order < left_order, scores, low)
                part = jnp.maximum(part[:, 0:128], part[:, 128:256])
                row_acc[u] = jnp.maximum(row_acc[u], part) if seen[u] else part
                seen[u] = True
            if cols:
                part = jnp.where(left_order < right_order, scores, low)
                part = jnp.max(part.reshape(ROWS // 8, 8, ROWS), axis=0)
                col_best = part if col_best is None else jnp.maximum(col_best, part)
        if right_slots[r]:
            best = jnp.max(col_best, axis=0, keepdims=True)
            col_outs[r][...] = jnp.maximum(best, col_prior[r][...]) if has_cols[r] else best
    for u in range(n_left):
        if left_slots[u]:
            best = jnp.max(row_acc[u].T, axis=0, keepdims=True)
            row_outs[u][...] = jnp.maximum(best, row_prior[u][...]) if has_rows[u] else best


def compare(left, right, pairs, rows=None, cols=None):
    rows, cols = rows or {}, cols or {}
    left_names, right_names = list(left), list(right)
    tiles = [(left_names.index(a), right_names.index(b), m != "cols", m != "rows") for a, b, m in pairs]
    left_slots = [any(t[0] == i and t[2] for t in tiles) for i in range(len(left))]
    right_slots = [any(t[1] == i and t[3] for t in tiles) for i in range(len(right))]
    has_rows = [n in rows and s for n, s in zip(left_names, left_slots)]
    has_cols = [n in cols and s for n, s in zip(right_names, right_slots)]
    args = [*left.values(), *right.values()]
    args += [rows[n] for n, h in zip(left_names, has_rows) if h]
    args += [cols[n] for n, h in zip(right_names, has_cols) if h]
    n_out = sum(left_slots) + sum(right_slots)
    outs = pl.pallas_call(
        functools.partial(
            compare_kernel, left_slots, right_slots, tiles, len(left), len(right), has_rows, has_cols
        ),
        out_shape=[jax.ShapeDtypeStruct((1, ROWS), jnp.float32)] * n_out,
        in_specs=[pl.BlockSpec(memory_space=pltpu.VMEM)] * len(args),
        out_specs=[pl.BlockSpec(memory_space=pltpu.VMEM)] * n_out,
        scratch_shapes=[pltpu.VMEM((len(left), ROWS, 128), jnp.float32)],
        compiler_params=pltpu.CompilerParams(vmem_limit_bytes=24 * 1024 * 1024),
        cost_estimate=pl.CostEstimate(
            flops=2 * len(tiles) * ROWS * ROWS * WIDTH // 4, bytes_accessed=ROWS, transcendentals=0
        ),
    )(*args)
    outs = list(outs)
    new_rows = dict(rows)
    new_rows.update({n: outs.pop(0) for n, s in zip(left_names, left_slots) if s})
    new_cols = dict(cols)
    new_cols.update({n: outs.pop(0) for n, s in zip(right_names, right_slots) if s})
    return new_rows, new_cols


def after(value, *others):
    return lax.optimization_barrier((value, *others))[0]


def on_device(embeddings, cluster, row_index):
    modes = {"own": "cols"}
    modes.update({n: "rows" for n in ("two_a", "two_b", "turn_a", "turn_b", "double")})

    def all_pairs(a, b):
        return [(u, v, modes.get(v, "both")) for v in b for u in a]

    own = pack(embeddings, cluster, row_index)
    twin = swap(own)
    step_a = fetch(own, (0, 1, 0), (0, 0, 1))
    near_a = fetch(own, (1, 0, 0), (-1, 0, 0))
    step_b = fetch(twin, (0, 1, 0), (0, 0, 1))
    near_b = fetch(twin, (1, 0, 0), (-1, 0, 0))
    two_a = fetch(step_a, (0, 1, 0), (0, 0, 1))
    turn_a = fetch(step_a, (0, 0, -1), (0, -1, 0))
    two_b = fetch(step_b, (0, 1, 0), (0, 0, 1))
    turn_b = fetch(step_b, (0, 0, -1), (0, -1, 0))
    far_a = swap(after(near_a, step_b))
    right = {"own": own, "step_a": step_a, "step_b": step_b, "turn_a": turn_a}
    left = {"own": own, "twin": twin, "near_a": near_a, "near_b": near_b}
    rows, cols = compare(left, right, all_pairs(left, right))
    first = rows["own"]
    across = fetch(after(near_a, step_a), (1, 0, 0), (-1, 0, 0))
    far_b = swap(after(near_b, far_a, turn_b, first))
    last_a = fetch(two_a, (0, 0, -1), (0, -1, 0))
    rest = {"far_a": far_a, "far_b": far_b}
    left = {**left, **rest}
    more = {"two_a": two_a, "turn_b": turn_b}
    rows, cols = compare(left, {**right, **more}, all_pairs(rest, right) + all_pairs(left, more), rows, cols)
    second = rows["own"]
    across_twin = swap(after(across, two_a, turn_a))
    corner = fetch(after(step_a, two_b, second), (0, 0, 1), (0, 1, 0))
    double = fetch(last_a, (0, 0, -1), (0, -1, 0))

    last_b = fetch(two_b, (0, 0, -1), (0, -1, 0))
    right = {**right, **more}
    rest = {"across": across, "across_twin": across_twin}
    left = {**left, **rest}
    more = {"two_b": two_b}
    rows, cols = compare(left, {**right, **more}, all_pairs(rest, right) + all_pairs(left, more), rows, cols)

    def both(name):
        return jnp.concatenate([cols[name + "_a"], cols[name + "_b"]], axis=0)

    step_back = give(both("step"), (0, 1, 0), (0, 0, 1))
    more = {"last_a": last_a, "double": double}
    rows, cols = compare(left, more, all_pairs(left, more), rows, cols)
    more = {"last_b": after(last_b, step_back), "corner": corner}
    rows, cols = compare(left, more, all_pairs(left, more), rows, cols)
    corner_back = give(cols["corner"], (0, 1, 1))
    last_back = give(both("last"), (0, 2, -1), (0, -1, 2))
    partner = swap(jnp.concatenate([rows["twin"], rows["far_a"], rows["far_b"], rows["across_twin"]], axis=0))
    own_rows = jnp.maximum(rows["own"], partner[0:1])
    near_rows = jnp.maximum(jnp.concatenate([rows["near_a"], rows["near_b"]], axis=0), partner[1:3])
    across_rows = jnp.maximum(rows["across"], partner[3:4])
    near_back = give(near_rows, (1, 0, 0), (-1, 0, 0))
    across_back = give(across_rows, (2, 0, 0))
    pairs = functools.reduce(jnp.maximum, [step_back, last_back, near_back])
    other = swap(pairs[1:2])
    best = functools.reduce(jnp.maximum, [cols["own"], own_rows, corner_back, across_back, pairs[0:1], other])
    return best.reshape(ROWS)


def solution(mesh):
    fine = Mesh(mesh.devices.reshape(SIZES), AXES)
    return jax.shard_map(
        on_device,
        mesh=fine,
        in_specs=(P(AXES, None), P(AXES), P(AXES)),
        out_specs=P(AXES),
        check_vma=False,
    )
```

```python
import functools

import jax
import jax.numpy as jnp
from jax import lax
from jax.experimental import pallas as pl
from jax.experimental.pallas import tpu as pltpu
from jax.sharding import Mesh, PartitionSpec as P

CL_GROUP = 2
EPSILON = 1e-06
ROWS = 256
WIDTH = 1024
PAD = 16
SIZES = (4, 4, 4, 2)
AXES = ("x", "z", "y", "c")


def flat(x, z, y, c):
    return ((x % 4 * 4 + z % 4) * 4 + y % 4) * 2 + c


def fetch(unit, first, second=None):
    ahead = (first, first if second is None else second)
    route = []
    for i in range(4):
        for j in range(4):
            for k in range(4):
                for c in range(2):
                    x, y, z = ahead[c]
                    route.append((flat(i + x, j + z, k + y, c), flat(i, j, k, c)))
    return lax.ppermute(unit, AXES, route)


def give(values, first, second=None):
    return fetch(values, tuple(-v for v in first), tuple(-v for v in second or first))


def swap(unit):
    return lax.ppermute(unit, AXES, [(i ^ 1, i) for i in range(128)])


def pack_kernel(emb_ref, cluster_ref, index_ref, unit_ref):
    widened = emb_ref[...].astype(jnp.float32)
    scale = lax.rsqrt(jnp.sum(widened * widened, axis=1, keepdims=True) + EPSILON)
    unit_ref[0:ROWS, :] = (widened * scale).astype(jnp.bfloat16)
    cluster = cluster_ref[...]
    index = index_ref[...]
    high = lax.shift_right_logical(index, 8)
    low = index - high * 256
    ids = jnp.concatenate([low, high, cluster, jnp.zeros_like(low)], axis=1).astype(jnp.float32)
    ids = jnp.concatenate([ids, jnp.zeros((PAD - 1, WIDTH), jnp.float32)], axis=0)
    unit_ref[ROWS : ROWS + PAD, :] = ids.astype(jnp.bfloat16)


def pack(embeddings, cluster, row_index):
    return pl.pallas_call(
        pack_kernel,
        out_shape=pltpu.VMEM((ROWS + PAD, WIDTH), jnp.bfloat16),
        in_specs=[pl.BlockSpec(memory_space=pltpu.VMEM)] * 3,
        out_specs=pl.BlockSpec(memory_space=pltpu.VMEM),
        cost_estimate=pl.CostEstimate(flops=4 * ROWS * WIDTH, bytes_accessed=4 * ROWS * WIDTH, transcendentals=ROWS),
    )(embeddings, cluster.reshape(1, ROWS), row_index.reshape(1, ROWS))


def ids_of(unit_ref):
    ids = unit_ref[ROWS : ROWS + PAD, :].astype(jnp.float32)[0:1, :]
    order = ids[:, 256:512] * 256.0 + ids[:, 0:256]
    return ids[:, 512:768], order


def compare_kernel(left_slots, right_slots, tiles, n_left, n_right, has_rows, has_cols, *refs):
    left = refs[:n_left]
    right = refs[n_left : n_left + n_right]
    rest = list(refs[n_left + n_right :])
    row_prior = [rest.pop(0) if h else None for h in has_rows]
    col_prior = [rest.pop(0) if h else None for h in has_cols]
    row_outs = [rest.pop(0) if s else None for s in left_slots]
    col_outs = [rest.pop(0) if s else None for s in right_slots]
    row_acc = rest.pop(0)
    low = jnp.float32(-1.0)
    keys = []
    for u in range(n_left):
        cluster, order = ids_of(left[u])
        turned = jnp.concatenate([cluster, order, jnp.zeros((6, ROWS), jnp.float32)], axis=0).T
        keys.append((turned[:, 0:1], turned[:, 1:2]))
    seen = [False] * n_left
    for r in range(n_right):
        right_cluster, right_order = ids_of(right[r])
        col_best = None
        for u, v, rows, cols in tiles:
            if v != r:
                continue
            scores = lax.dot_general(
                left[u][0:ROWS, :], right[r][0:ROWS, :], (((1,), (1,)), ((), ())), preferred_element_type=jnp.float32
            )
            left_cluster, left_order = keys[u]
            scores = jnp.where(left_cluster == right_cluster, scores, low)
            if rows:
                part = jnp.where(right_order < left_order, scores, low)
                part = jnp.maximum(part[:, 0:128], part[:, 128:256])
                row_acc[u] = jnp.maximum(row_acc[u], part) if seen[u] else part
                seen[u] = True
            if cols:
                part = jnp.where(left_order < right_order, scores, low)
                part = jnp.max(part.reshape(ROWS // 8, 8, ROWS), axis=0)
                col_best = part if col_best is None else jnp.maximum(col_best, part)
        if right_slots[r]:
            best = jnp.max(col_best, axis=0, keepdims=True)
            col_outs[r][...] = jnp.maximum(best, col_prior[r][...]) if has_cols[r] else best
    for u in range(n_left):
        if left_slots[u]:
            best = jnp.max(row_acc[u].T, axis=0, keepdims=True)
            row_outs[u][...] = jnp.maximum(best, row_prior[u][...]) if has_rows[u] else best


def compare(left, right, pairs, rows=None, cols=None):
    rows, cols = rows or {}, cols or {}
    left_names, right_names = list(left), list(right)
    tiles = [(left_names.index(a), right_names.index(b), m != "cols", m != "rows") for a, b, m in pairs]
    left_slots = [any(t[0] == i and t[2] for t in tiles) for i in range(len(left))]
    right_slots = [any(t[1] == i and t[3] for t in tiles) for i in range(len(right))]
    has_rows = [n in rows and s for n, s in zip(left_names, left_slots)]
    has_cols = [n in cols and s for n, s in zip(right_names, right_slots)]
    args = [*left.values(), *right.values()]
    args += [rows[n] for n, h in zip(left_names, has_rows) if h]
    args += [cols[n] for n, h in zip(right_names, has_cols) if h]
    n_out = sum(left_slots) + sum(right_slots)
    outs = pl.pallas_call(
        functools.partial(
            compare_kernel, left_slots, right_slots, tiles, len(left), len(right), has_rows, has_cols
        ),
        out_shape=[jax.ShapeDtypeStruct((1, ROWS), jnp.float32)] * n_out,
        in_specs=[pl.BlockSpec(memory_space=pltpu.VMEM)] * len(args),
        out_specs=[pl.BlockSpec(memory_space=pltpu.VMEM)] * n_out,
        scratch_shapes=[pltpu.VMEM((len(left), ROWS, 128), jnp.float32)],
        compiler_params=pltpu.CompilerParams(vmem_limit_bytes=24 * 1024 * 1024),
        cost_estimate=pl.CostEstimate(
            flops=2 * len(tiles) * ROWS * ROWS * WIDTH // 4, bytes_accessed=ROWS, transcendentals=0
        ),
    )(*args)
    outs = list(outs)
    new_rows = dict(rows)
    new_rows.update({n: outs.pop(0) for n, s in zip(left_names, left_slots) if s})
    new_cols = dict(cols)
    new_cols.update({n: outs.pop(0) for n, s in zip(right_names, right_slots) if s})
    return new_rows, new_cols


def after(value, *others):
    return lax.optimization_barrier((value, *others))[0]


def on_device(embeddings, cluster, row_index):
    modes = {"own": "cols"}
    modes.update({n: "rows" for n in ("two_a", "two_b", "turn_a", "turn_b", "double")})

    def all_pairs(a, b):
        return [(u, v, modes.get(v, "both")) for v in b for u in a]

    own = pack(embeddings, cluster, row_index)
    twin = swap(own)
    step_a = fetch(own, (0, 1, 0), (0, 0, 1))
    near_a = fetch(own, (1, 0, 0), (-1, 0, 0))
    step_b = fetch(twin, (0, 1, 0), (0, 0, 1))
    near_b = fetch(twin, (1, 0, 0), (-1, 0, 0))
    two_a = fetch(step_a, (0, 1, 0), (0, 0, 1))
    turn_a = fetch(step_a, (0, 0, -1), (0, -1, 0))
    two_b = fetch(step_b, (0, 1, 0), (0, 0, 1))
    turn_b = fetch(step_b, (0, 0, -1), (0, -1, 0))
    far_a = swap(after(near_a, step_b))
    right = {"own": own, "step_a": step_a, "step_b": step_b, "turn_a": turn_a}
    left = {"own": own, "twin": twin, "near_a": near_a, "near_b": near_b}
    rows, cols = compare(left, right, all_pairs(left, right))
    first = rows["own"]
    across = fetch(after(near_a, step_a), (1, 0, 0), (-1, 0, 0))
    far_b = swap(after(near_b, far_a, turn_b, first))
    last_a = fetch(two_a, (0, 0, -1), (0, -1, 0))
    rest = {"far_a": far_a, "far_b": far_b}
    left = {**left, **rest}
    more = {"two_a": two_a, "turn_b": turn_b}
    rows, cols = compare(left, {**right, **more}, all_pairs(rest, right) + all_pairs(left, more), rows, cols)
    second = rows["own"]
    across_twin = swap(after(across, two_a, turn_a))
    corner = fetch(after(step_a, two_b, second), (0, 0, 1), (0, 1, 0))
    double = fetch(last_a, (0, 0, -1), (0, -1, 0))

    last_b = fetch(two_b, (0, 0, -1), (0, -1, 0))
    right = {**right, **more}
    rest = {"across": across, "across_twin": across_twin}
    left = {**left, **rest}
    more = {"two_b": two_b, "last_a": last_a}
    rows, cols = compare(left, {**right, **more}, all_pairs(rest, right) + all_pairs(left, more), rows, cols)

    def both(name):
        return jnp.concatenate([cols[name + "_a"], cols[name + "_b"]], axis=0)

    step_back = give(both("step"), (0, 1, 0), (0, 0, 1))
    more = {"double": double}
    rows, cols = compare(left, more, all_pairs(left, more), rows, cols)
    more = {"last_b": after(last_b, step_back), "corner": corner}
    rows, cols = compare(left, more, all_pairs(left, more), rows, cols)
    corner_back = give(cols["corner"], (0, 1, 1))
    last_back = give(both("last"), (0, 2, -1), (0, -1, 2))
    partner = swap(jnp.concatenate([rows["twin"], rows["far_a"], rows["far_b"], rows["across_twin"]], axis=0))
    own_rows = jnp.maximum(rows["own"], partner[0:1])
    near_rows = jnp.maximum(jnp.concatenate([rows["near_a"], rows["near_b"]], axis=0), partner[1:3])
    across_rows = jnp.maximum(rows["across"], partner[3:4])
    near_back = give(near_rows, (1, 0, 0), (-1, 0, 0))
    across_back = give(across_rows, (2, 0, 0))
    pairs = functools.reduce(jnp.maximum, [step_back, last_back, near_back])
    other = swap(pairs[1:2])
    best = functools.reduce(jnp.maximum, [cols["own"], own_rows, corner_back, across_back, pairs[0:1], other])
    return best.reshape(ROWS)


def solution(mesh):
    fine = Mesh(mesh.devices.reshape(SIZES), AXES)
    return jax.shard_map(
        on_device,
        mesh=fine,
        in_specs=(P(AXES, None), P(AXES), P(AXES)),
        out_specs=P(AXES),
        check_vma=False,
    )
```
